32 devices in a mesh: blk: 8 (over z, x), rep: 4 (over y, core).
Axes of the slice: x: 2, y: 2, z: 4, core: 2. Of those that a mesh axis runs over, the one named last changes fastest.
Arguments:
- image_embed: bfloat16 [4, 192, 1280], P('rep', 'blk'), may hold values from -12 to 12
- text_hidden: bfloat16 [4, 192, 640], P('rep', 'blk'), may hold values from -6 to 6
- text_rest: bfloat16 [4, 192, 1280], P('rep', 'blk'), may hold values from -52 to 52
- proj_window: bfloat16 [640, 1280], P('blk'), may hold values from -0.15625 to 0.15625
- log_scale: float32 [1], replicated, may hold values from 4.66 to 5
Outputs:
- loss: float32 [1], replicated
- grad_log_scale: float32 [1], replicated
- grad_image: bfloat16 [4, 192, 1280], P('rep', 'blk')
- grad_text: bfloat16 [4, 192, 1280], P('rep', 'blk')
- grad_proj: float32 [640, 1280], P('blk')
The draws below stay inside these ranges and needn't reach their ends.
All inputs are finite; a program needn't handle non-finite values.
Results may differ from the reference program's by a relative error of at most 0.01.
Values may be sent and summed in bfloat16 or wider, within the bound.
No kernel may reach another device: no remote copies, remote signals or barrier semaphores. Data moves between devices by JAX's collectives and lax.ppermute only.
A program may use at most 64 MiB of HBM per device.

```python
import jax
import jax.numpy as jnp
from jax import lax

E = 1280
DT_WIN = 640
GROUP = 192
REPLICAS = 4


def shared_image(key, low_end, high_end):
    rough_part = jnp.clip(jax.random.normal(jax.random.fold_in(key, 12), (REPLICAS, GROUP, E), jnp.float32), -6.0, 6.0)
    log_low = jnp.log(jnp.float32(low_end))
    log_high = jnp.log(jnp.float32(high_end))
    row_scale = jnp.exp(jax.random.uniform(jax.random.fold_in(key, 13), (REPLICAS, GROUP, 1), jnp.float32, log_low, log_high))
    unscaled = rough_part
    return unscaled * row_scale


def draw_image_embed(key, part):
    scaled = shared_image(key, 1.0, 1.0)
    return scaled.astype(jnp.bfloat16)


def draw_text_rest(key, part):
    own_key = jax.random.fold_in(key, 5)
    base_part = 0.7 * jnp.clip(jax.random.normal(jax.random.fold_in(own_key, 1), (REPLICAS, GROUP, E), jnp.float32), -5.0 / 0.7, 5.0 / 0.7)
    return base_part.astype(jnp.bfloat16)


def block_scale(rng, dims, shards, low, high):
    level = 1.0
    for axis_at, blocks in shards:
        steps = jax.random.uniform(jax.random.fold_in(jax.random.fold_in(rng, 6), axis_at), (blocks,), jnp.float32, low / len(shards), high / len(shards))
        level = level * jnp.repeat(jnp.exp(steps), dims[axis_at] // blocks).reshape((-1,) + (1,) * (len(dims) - 1 - axis_at))
    return level


def centred(rng, extent, scale, bound, pieces=(), kind=jnp.bfloat16):
    level = block_scale(rng, extent, pieces, -0.22, 0.18) if pieces else 1.0
    result = jax.random.normal(rng, extent, jnp.float32) * scale * level
    return jnp.minimum(jnp.maximum(result, -bound), bound).astype(kind)


def setup_inputs(seed: int = 0) -> dict:
    seeds = jax.random.split(jax.random.key(seed), 6)
    return {
        "image_embed": draw_image_embed(jax.random.fold_in(seeds[5], 71), 0),
        "text_hidden": centred(seeds[1], (REPLICAS, GROUP, DT_WIN), 1.0, 6.0, ((0, 4), (1, 8))),
        "text_rest": draw_text_rest(jax.random.fold_in(seeds[5], 71), 0),
        "proj_window": centred(seeds[3], (DT_WIN, E), (2 * DT_WIN) ** -0.5, 0.15625, ((0, 8),)),
        "log_scale": jnp.clip(jax.random.uniform(seeds[4], (1,), jnp.float32, 4.66, 5.0), 4.66, 5.0),
    }


def unit_rows(values):
    row_norm = jnp.sqrt(lax.optimization_barrier(jnp.sum(values * values, axis=-1, keepdims=True)) + 1e-06)
    return (values / row_norm, row_norm)

def unit_back(unit_vec, row_norm, grad_unit):
    return (grad_unit - unit_vec * lax.optimization_barrier(jnp.sum(unit_vec * grad_unit, axis=-1, keepdims=True))) / row_norm

def reference(image_embed, text_hidden, text_rest, proj_window, log_scale):
    logit_scale = jnp.exp(log_scale[0])
    factor = 1.0 / (2.0 * GROUP * REPLICAS)
    loss_total = jnp.float32(0.0)
    scale_total = jnp.float32(0.0)
    grad_images = []
    grad_texts = []
    grad_proj = jnp.zeros((DT_WIN, E), jnp.float32)
    diagonal_mask = jnp.eye(GROUP, dtype=jnp.float32)
    for replica in range(REPLICAS):
        text_embed = text_rest[replica].astype(jnp.float32) + jnp.dot(text_hidden[replica], proj_window, preferred_element_type=jnp.float32)
        text_unit, text_norm = unit_rows(text_embed)
        image_unit, image_norm = unit_rows(image_embed[replica].astype(jnp.float32))
        text_short = text_unit.astype(jnp.bfloat16)
        image_short = image_unit.astype(jnp.bfloat16)
        logits = logit_scale * jnp.dot(image_short, text_short.T, preferred_element_type=jnp.float32)
        row_lse = jax.nn.logsumexp(logits, axis=1)
        col_lse = jax.nn.logsumexp(logits, axis=0)
        loss_total = loss_total + factor * (jnp.sum(row_lse) + jnp.sum(col_lse) - 2.0 * jnp.sum(jnp.diagonal(logits)))
        coef = factor * (jnp.exp(logits - row_lse[:, None]) + jnp.exp(logits - col_lse[None, :]) - 2.0 * diagonal_mask)
        scale_total = scale_total + jnp.sum(coef * logits)
        coef_short = coef.astype(jnp.bfloat16)
        grad_image_unit = logit_scale * jnp.dot(coef_short, text_short, preferred_element_type=jnp.float32)
        grad_text_unit = logit_scale * jnp.dot(coef_short.T, image_short, preferred_element_type=jnp.float32)
        grad_images.append(unit_back(image_unit, image_norm, grad_image_unit).astype(jnp.bfloat16))
        grad_text = unit_back(text_unit, text_norm, grad_text_unit).astype(jnp.bfloat16)
        grad_texts.append(grad_text)
        grad_proj = grad_proj + jnp.dot(text_hidden[replica].T, grad_text, preferred_element_type=jnp.float32)
    return (loss_total.reshape(1), scale_total.reshape(1), jnp.stack(grad_images), jnp.stack(grad_texts), grad_proj)
```

```python
import functools

import jax
import jax.numpy as jnp
from jax import lax
from jax.experimental import pallas as pl
from jax.experimental.pallas import tpu as pltpu
from jax.sharding import PartitionSpec as P


def joined(value, axis, join):
    pieces = jax.tree.map(lambda part: lax.all_gather(part, axis), value)
    head = jax.tree.map(lambda part: part[0], pieces)
    tail = jax.tree.map(lambda part: part[1:], pieces)
    running, _ = lax.scan(lambda running, slab: (join(running, slab), None), head, tail)
    return running


def unit_rows(values):
    row_norm = jnp.sqrt(jnp.sum(values * values, axis=-1, keepdims=True) + 1e-06)
    return (values / row_norm, row_norm)


def unit_back(unit_vec, row_norm, grad_unit):
    return (grad_unit - unit_vec * jnp.sum(unit_vec * grad_unit, axis=-1, keepdims=True)) / row_norm


def pair_products(left, right):
    return lax.dot_general(
        left, right, (((1,), (1,)), ((), ())), preferred_element_type=jnp.float32
    )


def combine_parts(earlier, later):
    col_top = jnp.maximum(earlier[0], later[0])
    return (
        col_top,
        earlier[1] * jnp.exp(earlier[0] - col_top) + later[1] * jnp.exp(later[0] - col_top),
    )


def on_device(image_embed, text_hidden, text_rest, proj_window, log_scale):
    hidden = text_hidden[0]
    local_rows = hidden.shape[0]
    group_rows = local_rows * lax.axis_size("blk")
    offset = lax.axis_index("blk") * local_rows
    factor = 1.0 / (2.0 * group_rows * lax.axis_size("rep"))
    logit_scale = jnp.exp(log_scale[0])
    columns = hidden
    projected = jnp.dot(
        columns,
        lax.all_gather(proj_window, "blk", axis=0, tiled=True),
        preferred_element_type=jnp.float32,
    )
    text_unit, text_norm = unit_rows(text_rest[0].astype(jnp.float32) + projected)
    image_unit, image_norm = unit_rows(image_embed[0].astype(jnp.float32))
    text_short = text_unit.astype(jnp.bfloat16)
    image_short = image_unit.astype(jnp.bfloat16)
    all_text = lax.all_gather(text_short, "blk", axis=0, tiled=True)
    logits = logit_scale * pair_products(image_short, all_text)
    row_lse = jax.nn.logsumexp(logits, axis=1)
    col_max = jnp.max(logits, axis=0)
    col_sum = jnp.sum(jnp.exp(logits - col_max[None, :]), axis=0)
    col_top, col_total = joined((col_max, col_sum), "blk", combine_parts)
    col_lse = col_top + jnp.log(col_total)
    positions = lax.broadcasted_iota(jnp.int32, (local_rows, group_rows), 1)
    own_rows = lax.broadcasted_iota(jnp.int32, (local_rows, group_rows), 0) + offset
    diagonal_mask = (positions == own_rows).astype(jnp.float32)
    own_col = lax.dynamic_slice_in_dim(col_lse, offset, local_rows, 0)
    loss_local = factor * (
        jnp.sum(row_lse) + jnp.sum(own_col) - 2.0 * jnp.sum(diagonal_mask * logits)
    )
    coef_image = factor * (
        jnp.exp(logits - row_lse[:, None])
        + jnp.exp(logits - col_lse[None, :])
        - 2.0 * diagonal_mask
    )
    scale_local = jnp.sum(coef_image * logits)
    grad_image_unit = logit_scale * jnp.dot(
        coef_image.astype(jnp.bfloat16), all_text, preferred_element_type=jnp.float32
    )
    grad_image = unit_back(image_unit, image_norm, grad_image_unit).astype(jnp.bfloat16)
    row_all = lax.all_gather(row_lse, "blk", axis=0, tiled=True)
    all_image = lax.all_gather(image_short, "blk", axis=0, tiled=True)
    cross_logits = logit_scale * pair_products(text_short, all_image)
    coef_text = factor * (
        jnp.exp(cross_logits - row_all[None, :])
        + jnp.exp(cross_logits - own_col[:, None])
        - 2.0 * diagonal_mask
    )
    grad_text_unit = logit_scale * jnp.dot(
        coef_text.astype(jnp.bfloat16), all_image, preferred_element_type=jnp.float32
    )
    grad_text = unit_back(text_unit, text_norm, grad_text_unit).astype(jnp.bfloat16)
    columns = hidden
    grad_share = lax.psum_scatter(
        lax.dot_general(
            columns, grad_text, (((0,), (0,)), ((), ())), preferred_element_type=jnp.float32
        ),
        "blk",
        scatter_dimension=0,
        tiled=True,
    )
    grad_proj = lax.psum(grad_share, "rep")
    loss_value, scale_grad = lax.psum((loss_local, scale_local), ("blk", "rep"))
    return (
        loss_value.reshape(1),
        scale_grad.reshape(1),
        grad_image[None],
        grad_text[None],
        grad_proj,
    )


F32 = jnp.float32
BF16 = jnp.bfloat16
ROWWISE = (((1,), (1,)), ((), ()))
IN_VMEM = pl.BlockSpec(memory_space=pltpu.VMEM)
IN_SMEM = pl.BlockSpec(memory_space=pltpu.SMEM)


def number(z, x, y, core):
    return (z * 2 + x) * 4 + y * 2 + core


def moved(value, to):
    places = [(z, x, y, core) for z in range(4) for x in range(2) for y in range(2) for core in range(2)]
    return lax.ppermute(
        value, ("blk", "rep"), [(number(*place), number(*to(*place))) for place in places]
    )


def z_near(value):
    return moved(value, lambda z, x, y, core: (z ^ 1, x, y, core))


def z_far(value):
    return moved(value, lambda z, x, y, core: (z ^ 2, x, y, core))


def x_peer(value):
    return moved(value, lambda z, x, y, core: (z, 1 - x, y, core))


def y_peer(value):
    return moved(value, lambda z, x, y, core: (z, x, 1 - y, core))


def core_peer(value):
    return moved(value, lambda z, x, y, core: (z, x, y, 1 - core))


def regroup(value):
    return moved(value, lambda z, x, y, core: (z, core, y, x))


def in_parts(value):
    high = value.astype(BF16)
    rest = value - high.astype(F32)
    middle = rest.astype(BF16)
    return high, middle, (rest - middle.astype(F32)).astype(BF16)


def lanes_of(values, shape):
    lane = lax.broadcasted_iota(jnp.int32, shape, 1)
    row = jnp.zeros(shape, F32)
    for at, value in enumerate(values):
        row = jnp.where(lane == at, value.astype(F32), row)
    return row


def inverse_norm(values):
    return lax.rsqrt(jnp.sum(values * values, axis=-1, keepdims=True) + 1e-06)


def group_kernel(factor, place, log_scale, *refs):
    own_rows, peer_rows, own_proj, peer_proj = refs[:4], refs[4:8], refs[8:12], refs[12:16]
    keep, send, grads = refs[16:19]
    image, text, hidden, hidden_t, norms, proj, coefs, grad_all, grad_cols, share = refs[19:]
    z, x, core = place[0], place[1], place[2]
    rows, depth = own_rows[0].shape[0], own_proj[0].shape[1]
    width = image.shape[1]
    half = width // 2
    for side, (groups, projs) in enumerate(((own_rows, own_proj), (peer_rows, peer_proj))):
        for step in range(4):
            start = pl.multiple_of(((z ^ step) * 2 + (core ^ side)) * rows, 8)
            block = groups[step]
            image[pl.ds(start, rows), :] = block[:, :width].astype(F32)
            text[pl.ds(start, rows), :] = block[:, width : 2 * width].astype(F32)
            hidden[pl.ds(start, rows), :] = block[:, 2 * width :].astype(F32)
            for column in range(2):
                start = pl.multiple_of(((z ^ step) * 2 + (x ^ column)) * depth, 16)
                proj[core ^ side, pl.ds(start, depth), :] = projs[step][column]
    hidden_short = hidden[...].astype(BF16)
    for side in range(2):
        text[:, side * half : (side + 1) * half] += jnp.dot(
            hidden_short, proj[side], preferred_element_type=F32
        )
    hidden_t[...] = hidden[...].T
    text_inv = inverse_norm(text[...])
    text[...] = text[...] * text_inv
    text_short = text[...].astype(BF16)
    image_inv = inverse_norm(image[...])
    norms[...] = jnp.broadcast_to(image_inv, norms.shape)
    image[...] = image[...] * image_inv
    image_short = image[...].astype(BF16)
    scale = jnp.exp(jnp.full((1, 1), log_scale[0], F32))
    logits = scale * lax.dot_general(
        image_short, text_short, ROWWISE, preferred_element_type=F32
    )
    row_max = jnp.max(logits, axis=1, keepdims=True)
    row_lse = row_max + jnp.log(jnp.sum(jnp.exp(logits - row_max), axis=1, keepdims=True))
    col_max = jnp.max(logits, axis=0, keepdims=True)
    col_lse = col_max + jnp.log(jnp.sum(jnp.exp(logits - col_max), axis=0, keepdims=True))
    eye = (
        lax.broadcasted_iota(jnp.int32, logits.shape, 0)
        == lax.broadcasted_iota(jnp.int32, logits.shape, 1)
    ).astype(F32)
    coef = factor * (jnp.exp(logits - row_lse) + jnp.exp(logits - col_lse) - 2.0 * eye)
    loss = factor * (
        jnp.sum(row_lse, axis=0, keepdims=True)
        + jnp.sum(col_lse, axis=1, keepdims=True)
        - 2.0 * jnp.sum(jnp.sum(eye * logits, axis=1, keepdims=True), axis=0, keepdims=True)
    )
    scale_grad = jnp.sum(jnp.sum(coef * logits, axis=1, keepdims=True), axis=0, keepdims=True)
    coefs[...] = coef
    own = pl.multiple_of((z * 2 + core) * rows, 8)
    grad_unit = scale * jnp.dot(
        coefs[pl.ds(own, rows), :].astype(BF16), text_short, preferred_element_type=F32
    )
    unit = image[pl.ds(own, rows), :]
    grads[0] = (
        (grad_unit - unit * jnp.sum(unit * grad_unit, axis=-1, keepdims=True))
        * norms[pl.ds(own, rows), :1]
    ).astype(BF16)
    grad_unit = scale * jnp.dot(coef.T.astype(BF16), image_short, preferred_element_type=F32)
    unit = text[...]
    grad_all[...] = (
        grad_unit - unit * jnp.sum(unit * grad_unit, axis=-1, keepdims=True)
    ) * text_inv
    grads[1] = grad_all[pl.ds(own, rows), :].astype(BF16)
    for side in range(2):
        grad_cols[side] = grad_all[:, side * half : (side + 1) * half].astype(BF16)
    share[...] = jnp.dot(
        hidden_t[pl.ds(pl.multiple_of(z * 2 * depth, 8), 2 * depth), :].astype(BF16),
        grad_cols[core],
        preferred_element_type=F32,
    )
    keep[:depth, :] = share[pl.ds(pl.multiple_of(x * depth, 8), depth), :]
    keep[depth:, :] = lanes_of((loss, scale_grad), (8, half))
    send[:depth, :] = share[pl.ds(pl.multiple_of((1 - x) * depth, 8), depth), :].astype(BF16)
    send[depth:, :] = lanes_of(in_parts(loss) + in_parts(scale_grad), (16, half)).astype(BF16)


def total_of(parts):
    parts = parts.astype(F32)
    return (
        parts[:, 0:1] + parts[:, 1:2] + parts[:, 2:3],
        parts[:, 3:4] + parts[:, 4:5] + parts[:, 5:6],
    )


def fold_x(keep, received, send):
    depth = keep.shape[0] - 8
    send[:depth, :] = (keep[:depth, :] + received[:depth, :].astype(F32)).astype(BF16)
    totals = total_of(received[depth:, :])
    parts = ()
    for at in range(2):
        parts += in_parts(keep[depth : depth + 1, at : at + 1] + totals[at][:1])
    send[depth:, :] = lanes_of(parts, (16, keep.shape[1])).astype(BF16)


def fold_y(sent, received, share, totals):
    depth = share.shape[0]
    share[...] = sent[:depth, :].astype(F32) + received[:depth, :].astype(F32)
    ours, theirs = total_of(sent[depth:, :]), total_of(received[depth:, :])
    totals[...] = lanes_of([(ours[at] + theirs[at])[:1] for at in range(2)], totals.shape)


def joined_halves(place, ours, theirs, out):
    half = ours.shape[1]
    for side in range(2):
        @pl.when(place[2] == side)
        def _():
            out[:, side * half : (side + 1) * half] = ours[...]
            out[:, (1 - side) * half : (2 - side) * half] = theirs[...]


def on_device_whole_group(image_embed, text_hidden, text_rest, proj_window, log_scale):
    rows, width = image_embed.shape[1:]
    depth = proj_window.shape[0]
    total_rows, total_depth, half = rows * 8, depth * 8, width // 2
    factor = 1.0 / (2.0 * total_rows * lax.axis_size("rep"))
    blk, rep = lax.axis_index("blk"), lax.axis_index("rep")
    z, x, core = blk // 2, blk % 2, rep % 2
    place = jnp.stack([z, x, core]).astype(jnp.int32)

    def own_and_z(value):
        far = z_far(value)
        return value, z_near(value), far, z_near(far)

    our_half = lax.dynamic_slice_in_dim(proj_window, core * half, half, 1)
    columns = jnp.stack(own_and_z(our_half))
    our_proj = jnp.stack([columns, x_peer(columns)], axis=1)
    their_proj = core_peer(our_proj)
    samples = jnp.concatenate([image_embed[0], text_rest[0], text_hidden[0]], axis=1)
    our_rows = own_and_z(regroup(samples))
    their_rows = core_peer(jnp.stack(our_rows))

    keep, send, grads = pl.pallas_call(
        functools.partial(group_kernel, factor),
        out_shape=(
            jax.ShapeDtypeStruct((depth + 8, half), F32),
            jax.ShapeDtypeStruct((depth + 16, half), BF16),
            jax.ShapeDtypeStruct((2, rows, width), BF16),
        ),
        in_specs=[IN_SMEM] * 2 + [IN_VMEM] * 16,
        out_specs=[IN_VMEM] * 3,
        scratch_shapes=[
            pltpu.VMEM((total_rows, width), F32),
            pltpu.VMEM((total_rows, width), F32),
            pltpu.VMEM((total_rows, total_depth), F32),
            pltpu.VMEM((total_depth, total_rows), F32),
            pltpu.VMEM((total_rows, 128), F32),
            pltpu.VMEM((2, total_depth, half), BF16),
            pltpu.VMEM((total_rows, total_rows), F32),
            pltpu.VMEM((total_rows, width), F32),
            pltpu.VMEM((2, total_rows, half), BF16),
            pltpu.VMEM((2 * depth, half), F32),
        ],
        compiler_params=pltpu.CompilerParams(vmem_limit_bytes=40 * 2**20),
        name="group_kernel",
    )(
        place,
        log_scale,
        *our_rows,
        *(their_rows[step] for step in range(4)),
        *(our_proj[step] for step in range(4)),
        *(their_proj[step] for step in range(4)),
    )
    grads = regroup(grads)
    folded = pl.pallas_call(
        fold_x,
        out_shape=jax.ShapeDtypeStruct(send.shape, BF16),
        in_specs=[IN_VMEM] * 2,
        out_specs=IN_VMEM,
        name="fold_x",
    )(keep, x_peer(send))
    share, totals = pl.pallas_call(
        fold_y,
        out_shape=(
            jax.ShapeDtypeStruct((depth, half), F32),
            jax.ShapeDtypeStruct((8, 128), F32),
        ),
        in_specs=[IN_VMEM] * 2,
        out_specs=[IN_VMEM] * 2,
        name="fold_y",
    )(folded, y_peer(folded))
    grad_proj = pl.pallas_call(
        joined_halves,
        out_shape=jax.ShapeDtypeStruct((depth, width), F32),
        in_specs=[IN_SMEM] + [IN_VMEM] * 2,
        out_specs=IN_VMEM,
        name="joined_halves",
    )(place, share, core_peer(share))
    return totals[0, 0:1], totals[0, 1:2], grads[0][None], grads[1][None], grad_proj


def solution(mesh):
    sizes = dict(mesh.shape)
    whole_group = sizes["blk"] == 8 and sizes["rep"] == 4
    return jax.shard_map(
        on_device_whole_group if whole_group else on_device,
        mesh=mesh,
        in_specs=(
            P("rep", "blk", None),
            P("rep", "blk", None),
            P("rep", "blk", None),
            P("blk", None),
            P(),
        ),
        out_specs=(P(), P(), P("rep", "blk", None), P("rep", "blk", None), P("blk", None)),
        check_vma=False,
    )
```

```python
import functools

import jax
import jax.numpy as jnp
from jax import lax
from jax.experimental import pallas as pl
from jax.experimental.pallas import tpu as pltpu
from jax.sharding import PartitionSpec as P


def joined(value, axis, join):
    pieces = jax.tree.map(lambda part: lax.all_gather(part, axis), value)
    head = jax.tree.map(lambda part: part[0], pieces)
    tail = jax.tree.map(lambda part: part[1:], pieces)
    running, _ = lax.scan(lambda running, slab: (join(running, slab), None), head, tail)
    return running


def unit_rows(values):
    row_norm = jnp.sqrt(jnp.sum(values * values, axis=-1, keepdims=True) + 1e-06)
    return (values / row_norm, row_norm)


def unit_back(unit_vec, row_norm, grad_unit):
    return (grad_unit - unit_vec * jnp.sum(unit_vec * grad_unit, axis=-1, keepdims=True)) / row_norm


def pair_products(left, right):
    return lax.dot_general(
        left, right, (((1,), (1,)), ((), ())), preferred_element_type=jnp.float32
    )


def combine_parts(earlier, later):
    col_top = jnp.maximum(earlier[0], later[0])
    return (
        col_top,
        earlier[1] * jnp.exp(earlier[0] - col_top) + later[1] * jnp.exp(later[0] - col_top),
    )


def on_device(image_embed, text_hidden, text_rest, proj_window, log_scale):
    hidden = text_hidden[0]
    local_rows = hidden.shape[0]
    group_rows = local_rows * lax.axis_size("blk")
    offset = lax.axis_index("blk") * local_rows
    factor = 1.0 / (2.0 * group_rows * lax.axis_size("rep"))
    logit_scale = jnp.exp(log_scale[0])
    columns = hidden
    projected = jnp.dot(
        columns,
        lax.all_gather(proj_window, "blk", axis=0, tiled=True),
        preferred_element_type=jnp.float32,
    )
    text_unit, text_norm = unit_rows(text_rest[0].astype(jnp.float32) + projected)
    image_unit, image_norm = unit_rows(image_embed[0].astype(jnp.float32))
    text_short = text_unit.astype(jnp.bfloat16)
    image_short = image_unit.astype(jnp.bfloat16)
    all_text = lax.all_gather(text_short, "blk", axis=0, tiled=True)
    logits = logit_scale * pair_products(image_short, all_text)
    row_lse = jax.nn.logsumexp(logits, axis=1)
    col_max = jnp.max(logits, axis=0)
    col_sum = jnp.sum(jnp.exp(logits - col_max[None, :]), axis=0)
    col_top, col_total = joined((col_max, col_sum), "blk", combine_parts)
    col_lse = col_top + jnp.log(col_total)
    positions = lax.broadcasted_iota(jnp.int32, (local_rows, group_rows), 1)
    own_rows = lax.broadcasted_iota(jnp.int32, (local_rows, group_rows), 0) + offset
    diagonal_mask = (positions == own_rows).astype(jnp.float32)
    own_col = lax.dynamic_slice_in_dim(col_lse, offset, local_rows, 0)
    loss_local = factor * (
        jnp.sum(row_lse) + jnp.sum(own_col) - 2.0 * jnp.sum(diagonal_mask * logits)
    )
    coef_image = factor * (
        jnp.exp(logits - row_lse[:, None])
        + jnp.exp(logits - col_lse[None, :])
        - 2.0 * diagonal_mask
    )
    scale_local = jnp.sum(coef_image * logits)
    grad_image_unit = logit_scale * jnp.dot(
        coef_image.astype(jnp.bfloat16), all_text, preferred_element_type=jnp.float32
    )
    grad_image = unit_back(image_unit, image_norm, grad_image_unit).astype(jnp.bfloat16)
    row_all = lax.all_gather(row_lse, "blk", axis=0, tiled=True)
    all_image = lax.all_gather(image_short, "blk", axis=0, tiled=True)
    cross_logits = logit_scale * pair_products(text_short, all_image)
    coef_text = factor * (
        jnp.exp(cross_logits - row_all[None, :])
        + jnp.exp(cross_logits - own_col[:, None])
        - 2.0 * diagonal_mask
    )
    grad_text_unit = logit_scale * jnp.dot(
        coef_text.astype(jnp.bfloat16), all_image, preferred_element_type=jnp.float32
    )
    grad_text = unit_back(text_unit, text_norm, grad_text_unit).astype(jnp.bfloat16)
    columns = hidden
    grad_share = lax.psum_scatter(
        lax.dot_general(
            columns, grad_text, (((0,), (0,)), ((), ())), preferred_element_type=jnp.float32
        ),
        "blk",
        scatter_dimension=0,
        tiled=True,
    )
    grad_proj = lax.psum(grad_share, "rep")
    loss_value, scale_grad = lax.psum((loss_local, scale_local), ("blk", "rep"))
    return (
        loss_value.reshape(1),
        scale_grad.reshape(1),
        grad_image[None],
        grad_text[None],
        grad_proj,
    )


F32 = jnp.float32
BF16 = jnp.bfloat16
ROWWISE = (((1,), (1,)), ((), ()))
IN_VMEM = pl.BlockSpec(memory_space=pltpu.VMEM)
IN_SMEM = pl.BlockSpec(memory_space=pltpu.SMEM)
PROJ_ORDER = ((0, 0), (0, 1), (1, 0), (2, 0), (1, 1), (2, 1), (3, 0), (3, 1))


def number(z, x, y, core):
    return (z * 2 + x) * 4 + y * 2 + core


def moved(value, to):
    places = [(z, x, y, core) for z in range(4) for x in range(2) for y in range(2) for core in range(2)]
    return lax.ppermute(
        value, ("blk", "rep"), [(number(*place), number(*to(*place))) for place in places]
    )


def z_near(value):
    return moved(value, lambda z, x, y, core: (z ^ 1, x, y, core))


def z_far(value):
    return moved(value, lambda z, x, y, core: (z ^ 2, x, y, core))


def x_peer(value):
    return moved(value, lambda z, x, y, core: (z, 1 - x, y, core))


def y_peer(value):
    return moved(value, lambda z, x, y, core: (z, x, 1 - y, core))


def core_peer(value):
    return moved(value, lambda z, x, y, core: (z, x, y, 1 - core))


def regroup(value):
    return moved(value, lambda z, x, y, core: (z, core, y, x))


def in_parts(value):
    high = value.astype(BF16)
    rest = value - high.astype(F32)
    middle = rest.astype(BF16)
    return high, middle, (rest - middle.astype(F32)).astype(BF16)


def lanes_of(values, group, shape):
    lane = lax.broadcasted_iota(jnp.int32, shape, 1)
    row = jnp.zeros(shape, F32)
    for at, value in enumerate(values):
        row = jnp.where(lane == at * 4 + group, value.astype(F32), row)
    return row


def inverse_norm(values):
    return lax.rsqrt(jnp.sum(values * values, axis=-1, keepdims=True) + 1e-06)


def group_kernel(factor, place, log_scale, *refs):
    rows_here, rows_there, projs = refs[:4], refs[4:8], refs[8:24]
    keep, send, grads = refs[24:27]
    image, text, hidden, hidden_t, norms, proj, coefs, grad_all, grad_cols, share = refs[27:]
    z, x, y, core = (place[at] for at in range(4))
    rows, depth = rows_here[0].shape[0], projs[0].shape[0]
    width = image.shape[1]
    half = width // 2
    for side, groups in enumerate((rows_here, rows_there)):
        for step in range(4):
            start = pl.multiple_of(((z ^ step) * 2 + (core ^ side)) * rows, 8)
            block = groups[step]
            image[pl.ds(start, rows), :] = block[:, :width].astype(F32)
            text[pl.ds(start, rows), :] = block[:, width : 2 * width].astype(F32)
            hidden[pl.ds(start, rows), :] = block[:, 2 * width :].astype(F32)
    for side in range(2):
        for at, (step, column) in enumerate(PROJ_ORDER):
            start = pl.multiple_of(((z ^ step) * 2 + (x ^ column)) * depth, 16)
            proj[core ^ side, pl.ds(start, depth), :] = projs[side * 8 + at][...]
    hidden_short = hidden[...].astype(BF16)
    for side in range(2):
        text[:, side * half : (side + 1) * half] += jnp.dot(
            hidden_short, proj[side], preferred_element_type=F32
        )
    hidden_t[...] = hidden[...].T
    text_inv = inverse_norm(text[...])
    text[...] = text[...] * text_inv
    text_short = text[...].astype(BF16)
    image_inv = inverse_norm(image[...])
    norms[...] = jnp.broadcast_to(image_inv, norms.shape)
    image[...] = image[...] * image_inv
    image_short = image[...].astype(BF16)
    scale = jnp.exp(jnp.full((1, 1), log_scale[0], F32))
    logits = scale * lax.dot_general(
        image_short, text_short, ROWWISE, preferred_element_type=F32
    )
    row_max = jnp.max(logits, axis=1, keepdims=True)
    row_lse = row_max + jnp.log(jnp.sum(jnp.exp(logits - row_max), axis=1, keepdims=True))
    col_max = jnp.max(logits, axis=0, keepdims=True)
    col_lse = col_max + jnp.log(jnp.sum(jnp.exp(logits - col_max), axis=0, keepdims=True))
    eye = (
        lax.broadcasted_iota(jnp.int32, logits.shape, 0)
        == lax.broadcasted_iota(jnp.int32, logits.shape, 1)
    ).astype(F32)
    coef = factor * (jnp.exp(logits - row_lse) + jnp.exp(logits - col_lse) - 2.0 * eye)
    loss = factor * (
        jnp.sum(row_lse, axis=0, keepdims=True)
        + jnp.sum(col_lse, axis=1, keepdims=True)
        - 2.0 * jnp.sum(jnp.sum(eye * logits, axis=1, keepdims=True), axis=0, keepdims=True)
    )
    scale_grad = jnp.sum(jnp.sum(coef * logits, axis=1, keepdims=True), axis=0, keepdims=True)
    coefs[...] = coef
    own = pl.multiple_of((z * 2 + core) * rows, 8)
    grad_unit = scale * jnp.dot(
        coefs[pl.ds(own, rows), :].astype(BF16), text_short, preferred_element_type=F32
    )
    unit = image[pl.ds(own, rows), :]
    grads[0] = (
        (grad_unit - unit * jnp.sum(unit * grad_unit, axis=-1, keepdims=True))
        * norms[pl.ds(own, rows), :1]
    ).astype(BF16)
    grad_unit = scale * jnp.dot(coef.T.astype(BF16), image_short, preferred_element_type=F32)
    unit = text[...]
    grad_all[...] = (
        grad_unit - unit * jnp.sum(unit * grad_unit, axis=-1, keepdims=True)
    ) * text_inv
    grads[1] = grad_all[pl.ds(own, rows), :].astype(BF16)
    for side in range(2):
        grad_cols[side] = grad_all[:, side * half : (side + 1) * half].astype(BF16)
    share[...] = jnp.dot(
        hidden_t[pl.ds(pl.multiple_of(z * 2 * depth, 8), 2 * depth), :].astype(BF16),
        grad_cols[core],
        preferred_element_type=F32,
    )
    totals = lanes_of(in_parts(loss) + in_parts(scale_grad), 2 * y + x, (16, half))
    keep[:depth, :] = share[pl.ds(pl.multiple_of(x * depth, 8), depth), :]
    keep[depth:, :] = totals
    send[:depth, :] = share[pl.ds(pl.multiple_of((1 - x) * depth, 8), depth), :].astype(BF16)
    send[depth:, :] = totals.astype(BF16)


def on_device_whole_group(image_embed, text_hidden, text_rest, proj_window, log_scale):
    rows, width = image_embed.shape[1:]
    depth = proj_window.shape[0]
    total_rows, total_depth, half = rows * 8, depth * 8, width // 2
    factor = 1.0 / (2.0 * total_rows * lax.axis_size("rep"))
    blk, rep = lax.axis_index("blk"), lax.axis_index("rep")
    z, x, y, core = blk // 2, blk % 2, rep // 2, rep % 2
    place = jnp.stack([z, x, y, core]).astype(jnp.int32)

    def own_and_z(value):
        far = z_far(value)
        return value, z_near(value), far, z_near(far)

    own_proj = lax.dynamic_slice_in_dim(proj_window, core * half, half, 1)
    far_proj, near_proj, x_proj = z_far(own_proj), z_near(own_proj), x_peer(own_proj)
    samples = jnp.concatenate([image_embed[0], text_rest[0], text_hidden[0]], axis=1)
    own_rows = regroup(samples)
    own_rows, near_proj = lax.optimization_barrier((own_rows, near_proj))
    far_rows, near_rows = z_far(own_rows), z_near(own_rows)
    last_proj = z_near(far_proj)
    x_near_proj, x_far_proj = x_peer(jnp.stack([near_proj, far_proj]))
    x_last_proj = x_peer(last_proj)
    last_rows = z_near(far_rows)
    rows_here = (own_rows, near_rows, far_rows, last_rows)
    rows_there = (
        core_peer(own_rows),
        *core_peer(jnp.stack([near_rows, far_rows])),
        core_peer(last_rows),
    )
    early_proj = (own_proj, x_proj, near_proj, far_proj)
    late_proj = (x_near_proj, x_far_proj, last_proj, x_last_proj)
    early_there = core_peer(jnp.stack(early_proj))
    late_there = core_peer(jnp.stack(late_proj))

    keep, send, grads = pl.pallas_call(
        functools.partial(group_kernel, factor),
        out_shape=(
            jax.ShapeDtypeStruct((depth + 16, half), F32),
            jax.ShapeDtypeStruct((depth + 16, half), BF16),
            jax.ShapeDtypeStruct((2, rows, width), BF16),
        ),
        in_specs=[IN_SMEM] * 2 + [IN_VMEM] * 24,
        out_specs=[IN_VMEM] * 3,
        scratch_shapes=[
            pltpu.VMEM((total_rows, width), F32),
            pltpu.VMEM((total_rows, width), F32),
            pltpu.VMEM((total_rows, total_depth), F32),
            pltpu.VMEM((total_depth, total_rows), F32),
            pltpu.VMEM((total_rows, 128), F32),
            pltpu.VMEM((2, total_depth, half), BF16),
            pltpu.VMEM((total_rows, total_rows), F32),
            pltpu.VMEM((total_rows, width), F32),
            pltpu.VMEM((2, total_rows, half), BF16),
            pltpu.VMEM((2 * depth, half), F32),
        ],
        compiler_params=pltpu.CompilerParams(vmem_limit_bytes=40 * 2**20),
        name="group_kernel",
    )(
        place,
        log_scale,
        *rows_here,
        *rows_there,
        *early_proj,
        *late_proj,
        *(early_there[at] for at in range(4)),
        *(late_there[at] for at in range(4)),
    )
    folded = (keep + x_peer(send).astype(F32)).astype(BF16)
    share = folded.astype(F32) + y_peer(folded).astype(F32)
    grads = regroup(grads)
    ours = share[:depth]
    theirs = core_peer(ours)
    grad_proj = jnp.where(
        core == 0,
        jnp.concatenate([ours, theirs], axis=1),
        jnp.concatenate([theirs, ours], axis=1),
    )
    totals = jnp.sum(share[depth, :24].reshape(2, 12), axis=1)
    return totals[0:1], totals[1:2], grads[0][None], grads[1][None], grad_proj


def solution(mesh):
    sizes = dict(mesh.shape)
    whole_group = sizes["blk"] == 8 and sizes["rep"] == 4
    return jax.shard_map(
        on_device_whole_group if whole_group else on_device,
        mesh=mesh,
        in_specs=(
            P("rep", "blk", None),
            P("rep", "blk", None),
            P("rep", "blk", None),
            P("blk", None),
            P(),
        ),
        out_specs=(P(), P(), P("rep", "blk", None), P("rep", "blk", None), P("blk", None)),
        check_vma=False,
    )
```

```python
import functools

import jax
import jax.numpy as jnp
from jax import lax
from jax.experimental import pallas as pl
from jax.experimental.pallas import tpu as pltpu
from jax.sharding import PartitionSpec as P


def joined(value, axis, join):
    pieces = jax.tree.map(lambda part: lax.all_gather(part, axis), value)
    head = jax.tree.map(lambda part: part[0], pieces)
    tail = jax.tree.map(lambda part: part[1:], pieces)
    running, _ = lax.scan(lambda running, slab: (join(running, slab), None), head, tail)
    return running


def unit_rows(values):
    row_norm = jnp.sqrt(jnp.sum(values * values, axis=-1, keepdims=True) + 1e-06)
    return (values / row_norm, row_norm)


def unit_back(unit_vec, row_norm, grad_unit):
    return (grad_unit - unit_vec * jnp.sum(unit_vec * grad_unit, axis=-1, keepdims=True)) / row_norm


def pair_products(left, right):
    return lax.dot_general(
        left, right, (((1,), (1,)), ((), ())), preferred_element_type=jnp.float32
    )


def combine_parts(earlier, later):
    col_top = jnp.maximum(earlier[0], later[0])
    return (
        col_top,
        earlier[1] * jnp.exp(earlier[0] - col_top) + later[1] * jnp.exp(later[0] - col_top),
    )


def on_device(image_embed, text_hidden, text_rest, proj_window, log_scale):
    hidden = text_hidden[0]
    local_rows = hidden.shape[0]
    group_rows = local_rows * lax.axis_size("blk")
    offset = lax.axis_index("blk") * local_rows
    factor = 1.0 / (2.0 * group_rows * lax.axis_size("rep"))
    logit_scale = jnp.exp(log_scale[0])
    columns = hidden
    projected = jnp.dot(
        columns,
        lax.all_gather(proj_window, "blk", axis=0, tiled=True),
        preferred_element_type=jnp.float32,
    )
    text_unit, text_norm = unit_rows(text_rest[0].astype(jnp.float32) + projected)
    image_unit, image_norm = unit_rows(image_embed[0].astype(jnp.float32))
    text_short = text_unit.astype(jnp.bfloat16)
    image_short = image_unit.astype(jnp.bfloat16)
    all_text = lax.all_gather(text_short, "blk", axis=0, tiled=True)
    logits = logit_scale * pair_products(image_short, all_text)
    row_lse = jax.nn.logsumexp(logits, axis=1)
    col_max = jnp.max(logits, axis=0)
    col_sum = jnp.sum(jnp.exp(logits - col_max[None, :]), axis=0)
    col_top, col_total = joined((col_max, col_sum), "blk", combine_parts)
    col_lse = col_top + jnp.log(col_total)
    positions = lax.broadcasted_iota(jnp.int32, (local_rows, group_rows), 1)
    own_rows = lax.broadcasted_iota(jnp.int32, (local_rows, group_rows), 0) + offset
    diagonal_mask = (positions == own_rows).astype(jnp.float32)
    own_col = lax.dynamic_slice_in_dim(col_lse, offset, local_rows, 0)
    loss_local = factor * (
        jnp.sum(row_lse) + jnp.sum(own_col) - 2.0 * jnp.sum(diagonal_mask * logits)
    )
    coef_image = factor * (
        jnp.exp(logits - row_lse[:, None])
        + jnp.exp(logits - col_lse[None, :])
        - 2.0 * diagonal_mask
    )
    scale_local = jnp.sum(coef_image * logits)
    grad_image_unit = logit_scale * jnp.dot(
        coef_image.astype(jnp.bfloat16), all_text, preferred_element_type=jnp.float32
    )
    grad_image = unit_back(image_unit, image_norm, grad_image_unit).astype(jnp.bfloat16)
    row_all = lax.all_gather(row_lse, "blk", axis=0, tiled=True)
    all_image = lax.all_gather(image_short, "blk", axis=0, tiled=True)
    cross_logits = logit_scale * pair_products(text_short, all_image)
    coef_text = factor * (
        jnp.exp(cross_logits - row_all[None, :])
        + jnp.exp(cross_logits - own_col[:, None])
        - 2.0 * diagonal_mask
    )
    grad_text_unit = logit_scale * jnp.dot(
        coef_text.astype(jnp.bfloat16), all_image, preferred_element_type=jnp.float32
    )
    grad_text = unit_back(text_unit, text_norm, grad_text_unit).astype(jnp.bfloat16)
    columns = hidden
    grad_share = lax.psum_scatter(
        lax.dot_general(
            columns, grad_text, (((0,), (0,)), ((), ())), preferred_element_type=jnp.float32
        ),
        "blk",
        scatter_dimension=0,
        tiled=True,
    )
    grad_proj = lax.psum(grad_share, "rep")
    loss_value, scale_grad = lax.psum((loss_local, scale_local), ("blk", "rep"))
    return (
        loss_value.reshape(1),
        scale_grad.reshape(1),
        grad_image[None],
        grad_text[None],
        grad_proj,
    )


F32 = jnp.float32
BF16 = jnp.bfloat16
ROWWISE = (((1,), (1,)), ((), ()))
IN_VMEM = pl.BlockSpec(memory_space=pltpu.VMEM)
IN_SMEM = pl.BlockSpec(memory_space=pltpu.SMEM)
ROW_STEPS = ((0, 1, 3, 2), (0, 2, 1, 3))
PROJ_STEPS = (((0, 2), 0), ((1, 3), 0), ((0, 2), 1), ((1, 3), 1))

def number(z, x, y, core):
    return (z * 2 + x) * 4 + y * 2 + core


def moved(value, to):
    places = [(z, x, y, core) for z in range(4) for x in range(2) for y in range(2) for core in range(2)]
    return lax.ppermute(
        value, ("blk", "rep"), [(number(*place), number(*to(*place))) for place in places]
    )


def z_near(value):
    return moved(value, lambda z, x, y, core: (z ^ 1, x, y, core))


def z_far(value):
    return moved(value, lambda z, x, y, core: (z ^ 2, x, y, core))


def x_peer(value):
    return moved(value, lambda z, x, y, core: (z, 1 - x, y, core))


def y_peer(value):
    return moved(value, lambda z, x, y, core: (z, x, 1 - y, core))


def xy_peer(value):
    return moved(value, lambda z, x, y, core: (z, 1 - x, 1 - y, core))


def core_peer(value):
    return moved(value, lambda z, x, y, core: (z, x, y, 1 - core))


def is_ahead(x, core):
    return x == core


def trade(z, x, y, core):
    return z, core, y, x


def first_move(value):
    return moved(value, lambda z, x, y, core: (z ^ 2, x, y, core) if is_ahead(x, core) else trade(z, x, y, core))


def second_move(value):
    return moved(value, lambda z, x, y, core: (z ^ 1 if is_ahead(x, core) else z ^ 2, x, y, core))


def fourth_move(value):
    return moved(value, lambda z, x, y, core: (z, x, 1 - y, core) if is_ahead(x, core) else (z ^ 1, x, y, core))


def trade_back(value):
    return moved(value, lambda z, x, y, core: (z ^ 1, x, y, core) if is_ahead(x, core) else trade(z, x, y, core))


def in_parts(value):
    high = value.astype(BF16)
    rest = value - high.astype(F32)
    middle = rest.astype(BF16)
    return high, middle, (rest - middle.astype(F32)).astype(BF16)


def lanes_of(values, group, shape):
    lane = lax.broadcasted_iota(jnp.int32, shape, 1)
    row = jnp.zeros(shape, F32)
    for at, value in enumerate(values):
        row = jnp.where(lane == at * 4 + group, value.astype(F32), row)
    return row


def inverse_norm(values):
    return lax.rsqrt(jnp.sum(values * values, axis=-1, keepdims=True) + 1e-06)


def group_kernel(factor, place, log_scale, *refs):
    rows_here, rows_there, projs = refs[:4], refs[4:8], refs[8:16]
    keep, send, grads = refs[16:19]
    image, text, hidden, hidden_t, norms, proj, coefs, grad_all, grad_cols, share = refs[19:]
    z, x, y, core = (place[at] for at in range(4))
    rows, depth = rows_here[0].shape[0], projs[0].shape[1]
    width = image.shape[1]
    half = width // 2
    ahead = is_ahead(x, core)
    for side, blocks in enumerate((rows_here, rows_there)):
        for block, *steps in zip(blocks, *ROW_STEPS):
            step = jnp.where(ahead, steps[side], steps[1 - side])
            start = pl.multiple_of(((z ^ step) * 2 + (core ^ side)) * rows, 8)
            image[pl.ds(start, rows), :] = block[:, :width].astype(F32)
            text[pl.ds(start, rows), :] = block[:, width : 2 * width].astype(F32)
            hidden[pl.ds(start, rows), :] = block[:, 2 * width :].astype(F32)
    for at, blocks in enumerate(projs):
        steps, column = PROJ_STEPS[at % 4]
        for block, step in enumerate(steps):
            start = pl.multiple_of(((z ^ step) * 2 + (x ^ column)) * depth, 16)
            proj[core ^ (at // 4), pl.ds(start, depth), :] = blocks[block]
    hidden_short = hidden[...].astype(BF16)
    for side in range(2):
        text[:, side * half : (side + 1) * half] += jnp.dot(
            hidden_short, proj[side], preferred_element_type=F32
        )
    hidden_t[...] = hidden[...].T
    text_inv = inverse_norm(text[...])
    text[...] = text[...] * text_inv
    text_short = text[...].astype(BF16)
    image_inv = inverse_norm(image[...])
    norms[...] = jnp.broadcast_to(image_inv, norms.shape)
    image[...] = image[...] * image_inv
    image_short = image[...].astype(BF16)
    scale = jnp.exp(jnp.full((1, 1), log_scale[0], F32))
    logits = scale * lax.dot_general(
        image_short, text_short, ROWWISE, preferred_element_type=F32
    )
    row_max = jnp.max(logits, axis=1, keepdims=True)
    row_lse = row_max + jnp.log(jnp.sum(jnp.exp(logits - row_max), axis=1, keepdims=True))
    col_max = jnp.max(logits, axis=0, keepdims=True)
    col_lse = col_max + jnp.log(jnp.sum(jnp.exp(logits - col_max), axis=0, keepdims=True))
    eye = (
        lax.broadcasted_iota(jnp.int32, logits.shape, 0)
        == lax.broadcasted_iota(jnp.int32, logits.shape, 1)
    ).astype(F32)
    coef = factor * (jnp.exp(logits - row_lse) + jnp.exp(logits - col_lse) - 2.0 * eye)
    loss = factor * (
        jnp.sum(row_lse, axis=0, keepdims=True)
        + jnp.sum(col_lse, axis=1, keepdims=True)
        - 2.0 * jnp.sum(jnp.sum(eye * logits, axis=1, keepdims=True), axis=0, keepdims=True)
    )
    scale_grad = jnp.sum(jnp.sum(coef * logits, axis=1, keepdims=True), axis=0, keepdims=True)
    coefs[...] = coef
    own = pl.multiple_of((z * 2 + core) * rows, 8)
    grad_unit = scale * jnp.dot(
        coefs[pl.ds(own, rows), :].astype(BF16), text_short, preferred_element_type=F32
    )
    unit = image[pl.ds(own, rows), :]
    grads[0] = (
        (grad_unit - unit * jnp.sum(unit * grad_unit, axis=-1, keepdims=True))
        * norms[pl.ds(own, rows), :1]
    ).astype(BF16)
    grad_unit = scale * jnp.dot(coef.T.astype(BF16), image_short, preferred_element_type=F32)
    unit = text[...]
    grad_all[...] = (
        grad_unit - unit * jnp.sum(unit * grad_unit, axis=-1, keepdims=True)
    ) * text_inv
    grads[1] = grad_all[pl.ds(own, rows), :].astype(BF16)
    for side in range(2):
        grad_cols[side] = grad_all[:, side * half : (side + 1) * half].astype(BF16)
    share[...] = jnp.dot(
        hidden_t[pl.ds(pl.multiple_of(z * 2 * depth, 8), 2 * depth), :].astype(BF16),
        grad_cols[core],
        preferred_element_type=F32,
    )
    totals = lanes_of(in_parts(loss) + in_parts(scale_grad), 2 * y + x, (16, half))
    keep[:depth, :] = share[pl.ds(pl.multiple_of(x * depth, 8), depth), :].astype(BF16)
    keep[depth:, :] = totals.astype(BF16)
    send[:depth, :] = share[pl.ds(pl.multiple_of((1 - x) * depth, 8), depth), :].astype(BF16)
    send[depth:, :] = totals.astype(BF16)


def on_device_whole_group(image_embed, text_hidden, text_rest, proj_window, log_scale):
    rows, width = image_embed.shape[1:]
    depth = proj_window.shape[0]
    total_rows, total_depth, half = rows * 8, depth * 8, width // 2
    factor = 1.0 / (2.0 * total_rows * lax.axis_size("rep"))
    blk, rep = lax.axis_index("blk"), lax.axis_index("rep")
    z, x, y, core = blk // 2, blk % 2, rep // 2, rep % 2
    place = jnp.stack([z, x, y, core]).astype(jnp.int32)

    def own_and_z(value):
        far = z_far(value)
        return value, z_near(value), far, z_near(far)

    ahead = is_ahead(x, core)
    own_proj = lax.dynamic_slice_in_dim(proj_window, core * half, half, 1)
    samples = jnp.concatenate([image_embed[0], text_rest[0], text_hidden[0]], axis=1)
    far_proj = z_far(own_proj)
    even = jnp.stack([own_proj, far_proj])
    (tied_first_0,), _ = lax.optimization_barrier(((samples,), far_proj))
    first = first_move(tied_first_0)
    own_rows = jnp.where(ahead, samples, first)
    second = second_move(own_rows)
    odd = z_near(even)
    even_across = x_peer(even)
    (tied_third_0,), _ = lax.optimization_barrier(((first,), even_across))
    third = z_near(tied_third_0)
    (tied_odd_across_0,), _ = lax.optimization_barrier(((odd,), first))
    odd_across = x_peer(tied_odd_across_0)
    (tied_fourth_0,), _ = lax.optimization_barrier(((second,), even_across))
    fourth = fourth_move(tied_fourth_0)
    fourth_rows = jnp.where(ahead, first, fourth)
    (tied_cg0_0, tied_cg0_1,), _ = lax.optimization_barrier(((own_rows, second,), odd))
    cg0 = core_peer(jnp.stack([tied_cg0_0, tied_cg0_1]))
    (tied_cg1_0, tied_cg1_1,), _ = lax.optimization_barrier(((third, fourth_rows,), even_across))
    cg1 = core_peer(jnp.stack([tied_cg1_0, tied_cg1_1]))
    cq0 = core_peer(jnp.stack([even, odd, even_across, odd_across]))
    rows_here = (own_rows, second, third, fourth_rows)
    rows_there = (cg0[0], cg0[1], cg1[0], cg1[1])
    proj_here = (even, odd, even_across, odd_across)
    proj_there = (cq0[0], cq0[1], cq0[2], cq0[3])

    keep, send, grads = pl.pallas_call(
        functools.partial(group_kernel, factor),
        out_shape=(
            jax.ShapeDtypeStruct((depth + 16, half), BF16),
            jax.ShapeDtypeStruct((depth + 16, half), BF16),
            jax.ShapeDtypeStruct((2, rows, width), BF16),
        ),
        in_specs=[IN_SMEM] * 2 + [IN_VMEM] * 16,
        out_specs=[IN_VMEM] * 3,
        scratch_shapes=[
            pltpu.VMEM((total_rows, width), F32),
            pltpu.VMEM((total_rows, width), F32),
            pltpu.VMEM((total_rows, total_depth), F32),
            pltpu.VMEM((total_depth, total_rows), F32),
            pltpu.VMEM((total_rows, 128), F32),
            pltpu.VMEM((2, total_depth, half), BF16),
            pltpu.VMEM((total_rows, total_rows), F32),
            pltpu.VMEM((total_rows, width), F32),
            pltpu.VMEM((2, total_rows, half), BF16),
            pltpu.VMEM((2 * depth, half), F32),
        ],
        compiler_params=pltpu.CompilerParams(vmem_limit_bytes=40 * 2**20),
        name="group_kernel",
    )(
        place,
        log_scale,
        *rows_here,
        *rows_there,
        *proj_here,
        *proj_there,
    )
    across = xy_peer(send).astype(F32)
    share = (keep.astype(F32) + y_peer(keep).astype(F32)) + (x_peer(send).astype(F32) + across)
    grads = jnp.where(is_ahead(x, core), grads, trade_back(grads))
    ours = share[:depth]
    theirs = core_peer(ours)
    grad_proj = jnp.where(
        core == 0,
        jnp.concatenate([ours, theirs], axis=1),
        jnp.concatenate([theirs, ours], axis=1),
    )
    totals = jnp.sum(share[depth, :24].reshape(2, 12), axis=1)
    return totals[0:1], totals[1:2], grads[0][None], grads[1][None], grad_proj


def solution(mesh):
    sizes = dict(mesh.shape)
    whole_group = sizes["blk"] == 8 and sizes["rep"] == 4
    return jax.shard_map(
        on_device_whole_group if whole_group else on_device,
        mesh=mesh,
        in_specs=(
            P("rep", "blk", None),
            P("rep", "blk", None),
            P("rep", "blk", None),
            P("blk", None),
            P(),
        ),
        out_specs=(P(), P(), P("rep", "blk", None), P("rep", "blk", None), P("blk", None)),
        check_vma=False,
    )
```

```python
import functools

import jax
import jax.numpy as jnp
from jax import lax
from jax.experimental import pallas as pl
from jax.experimental.pallas import tpu as pltpu
from jax.sharding import PartitionSpec as P


def joined(value, axis, join):
    pieces = jax.tree.map(lambda part: lax.all_gather(part, axis), value)
    head = jax.tree.map(lambda part: part[0], pieces)
    tail = jax.tree.map(lambda part: part[1:], pieces)
    running, _ = lax.scan(lambda running, slab: (join(running, slab), None), head, tail)
    return running


def unit_rows(values):
    row_norm = jnp.sqrt(jnp.sum(values * values, axis=-1, keepdims=True) + 1e-06)
    return (values / row_norm, row_norm)


def unit_back(unit_vec, row_norm, grad_unit):
    return (grad_unit - unit_vec * jnp.sum(unit_vec * grad_unit, axis=-1, keepdims=True)) / row_norm


def pair_products(left, right):
    return lax.dot_general(
        left, right, (((1,), (1,)), ((), ())), preferred_element_type=jnp.float32
    )


def combine_parts(earlier, later):
    col_top = jnp.maximum(earlier[0], later[0])
    return (
        col_top,
        earlier[1] * jnp.exp(earlier[0] - col_top) + later[1] * jnp.exp(later[0] - col_top),
    )


def on_device(image_embed, text_hidden, text_rest, proj_window, log_scale):
    hidden = text_hidden[0]
    local_rows = hidden.shape[0]
    group_rows = local_rows * lax.axis_size("blk")
    offset = lax.axis_index("blk") * local_rows
    factor = 1.0 / (2.0 * group_rows * lax.axis_size("rep"))
    logit_scale = jnp.exp(log_scale[0])
    columns = hidden
    projected = jnp.dot(
        columns,
        lax.all_gather(proj_window, "blk", axis=0, tiled=True),
        preferred_element_type=jnp.float32,
    )
    text_unit, text_norm = unit_rows(text_rest[0].astype(jnp.float32) + projected)
    image_unit, image_norm = unit_rows(image_embed[0].astype(jnp.float32))
    text_short = text_unit.astype(jnp.bfloat16)
    image_short = image_unit.astype(jnp.bfloat16)
    all_text = lax.all_gather(text_short, "blk", axis=0, tiled=True)
    logits = logit_scale * pair_products(image_short, all_text)
    row_lse = jax.nn.logsumexp(logits, axis=1)
    col_max = jnp.max(logits, axis=0)
    col_sum = jnp.sum(jnp.exp(logits - col_max[None, :]), axis=0)
    col_top, col_total = joined((col_max, col_sum), "blk", combine_parts)
    col_lse = col_top + jnp.log(col_total)
    positions = lax.broadcasted_iota(jnp.int32, (local_rows, group_rows), 1)
    own_rows = lax.broadcasted_iota(jnp.int32, (local_rows, group_rows), 0) + offset
    diagonal_mask = (positions == own_rows).astype(jnp.float32)
    own_col = lax.dynamic_slice_in_dim(col_lse, offset, local_rows, 0)
    loss_local = factor * (
        jnp.sum(row_lse) + jnp.sum(own_col) - 2.0 * jnp.sum(diagonal_mask * logits)
    )
    coef_image = factor * (
        jnp.exp(logits - row_lse[:, None])
        + jnp.exp(logits - col_lse[None, :])
        - 2.0 * diagonal_mask
    )
    scale_local = jnp.sum(coef_image * logits)
    grad_image_unit = logit_scale * jnp.dot(
        coef_image.astype(jnp.bfloat16), all_text, preferred_element_type=jnp.float32
    )
    grad_image = unit_back(image_unit, image_norm, grad_image_unit).astype(jnp.bfloat16)
    row_all = lax.all_gather(row_lse, "blk", axis=0, tiled=True)
    all_image = lax.all_gather(image_short, "blk", axis=0, tiled=True)
    cross_logits = logit_scale * pair_products(text_short, all_image)
    coef_text = factor * (
        jnp.exp(cross_logits - row_all[None, :])
        + jnp.exp(cross_logits - own_col[:, None])
        - 2.0 * diagonal_mask
    )
    grad_text_unit = logit_scale * jnp.dot(
        coef_text.astype(jnp.bfloat16), all_image, preferred_element_type=jnp.float32
    )
    grad_text = unit_back(text_unit, text_norm, grad_text_unit).astype(jnp.bfloat16)
    columns = hidden
    grad_share = lax.psum_scatter(
        lax.dot_general(
            columns, grad_text, (((0,), (0,)), ((), ())), preferred_element_type=jnp.float32
        ),
        "blk",
        scatter_dimension=0,
        tiled=True,
    )
    grad_proj = lax.psum(grad_share, "rep")
    loss_value, scale_grad = lax.psum((loss_local, scale_local), ("blk", "rep"))
    return (
        loss_value.reshape(1),
        scale_grad.reshape(1),
        grad_image[None],
        grad_text[None],
        grad_proj,
    )


F32 = jnp.float32
BF16 = jnp.bfloat16
ROWWISE = (((1,), (1,)), ((), ()))
IN_VMEM = pl.BlockSpec(memory_space=pltpu.VMEM)
IN_SMEM = pl.BlockSpec(memory_space=pltpu.SMEM)
ROW_STEPS = ((0, 1, 3, 2), (0, 2, 1, 3))
PROJ_STEPS = (((0, 2), 0), ((1,), 0), ((3,), 0), ((0, 2), 1), ((1, 3), 1))

def number(z, x, y, core):
    return (z * 2 + x) * 4 + y * 2 + core


def own_place():
    blk, rep = lax.axis_index("blk"), lax.axis_index("rep")
    return blk // 2, blk % 2, rep // 2, rep % 2


def moved(value, to):
    places = [(z, x, y, core) for z in range(4) for x in range(2) for y in range(2) for core in range(2)]
    return lax.ppermute(
        value, ("blk", "rep"), [(number(*place), number(*to(*place))) for place in places]
    )


def z_near(value):
    return moved(value, lambda z, x, y, core: (z ^ 1, x, y, core))


def z_far(value):
    return moved(value, lambda z, x, y, core: (z ^ 2, x, y, core))


def x_peer(value):
    return moved(value, lambda z, x, y, core: (z, 1 - x, y, core))


def y_peer(value):
    return moved(value, lambda z, x, y, core: (z, x, 1 - y, core))


def xy_peer(value):
    return moved(value, lambda z, x, y, core: (z, 1 - x, 1 - y, core))


def core_peer(value):
    return moved(value, lambda z, x, y, core: (z, x, y, 1 - core))


def is_ahead(x, core):
    return x == core


def trade(z, x, y, core):
    return z, core, y, x


def first_move(value):
    return moved(value, lambda z, x, y, core: (z ^ 2, x, y, core) if is_ahead(x, core) else trade(z, x, y, core))


def second_move(value):
    return moved(value, lambda z, x, y, core: (z ^ 1 if is_ahead(x, core) else z ^ 2, x, y, core))


def fourth_move(value):
    return moved(value, lambda z, x, y, core: (z, x, 1 - y, core) if is_ahead(x, core) else (z ^ 1, x, y, core))


def trade_back(value):
    return moved(value, lambda z, x, y, core: (z ^ 1, x, y, core) if is_ahead(x, core) else trade(z, x, y, core))


def in_parts(value):
    high = value.astype(BF16)
    rest = value - high.astype(F32)
    middle = rest.astype(BF16)
    return high, middle, (rest - middle.astype(F32)).astype(BF16)


def lanes_of(values, group, shape):
    lane = lax.broadcasted_iota(jnp.int32, shape, 1)
    row = jnp.zeros(shape, F32)
    for at, value in enumerate(values):
        row = jnp.where(lane == at * 4 + group, value.astype(F32), row)
    return row


def inverse_norm(values):
    return lax.rsqrt(jnp.sum(values * values, axis=-1, keepdims=True) + 1e-06)


def group_kernel(factor, log_scale, *refs):
    count = 2 * len(PROJ_STEPS)
    rows_here, rows_there, projs = refs[:4], refs[4:8], refs[8 : 8 + count]
    keep, send, grads = refs[8 + count : 11 + count]
    image, text, hidden, hidden_t, norms, proj, coefs, grad_all, grad_cols, share = refs[11 + count :]
    z, x, y, core = own_place()
    rows, depth = rows_here[0].shape[0], proj.shape[1] // 8
    width = image.shape[1]
    half = width // 2
    ahead = is_ahead(x, core)
    for side, blocks in enumerate((rows_here, rows_there)):
        for block, *steps in zip(blocks, *ROW_STEPS):
            step = jnp.where(ahead, steps[side], steps[1 - side])
            start = pl.multiple_of(((z ^ step) * 2 + (core ^ side)) * rows, 8)
            image[pl.ds(start, rows), :] = block[:, :width].astype(F32)
            text[pl.ds(start, rows), :] = block[:, width : 2 * width].astype(F32)
            hidden[pl.ds(start, rows), :] = block[:, 2 * width :].astype(F32)
    for at, blocks in enumerate(projs):
        side, kind = divmod(at, len(PROJ_STEPS))
        steps, column = PROJ_STEPS[kind]
        for block, step in enumerate(steps):
            start = pl.multiple_of(((z ^ step) * 2 + (x ^ column)) * depth, 16)
            proj[core ^ side, pl.ds(start, depth), :] = blocks[block]
    hidden_short = hidden[...].astype(BF16)
    for side in range(2):
        text[:, side * half : (side + 1) * half] += jnp.dot(
            hidden_short, proj[side], preferred_element_type=F32
        )
    hidden_t[...] = hidden[...].T
    text_inv = inverse_norm(text[...])
    text[...] = text[...] * text_inv
    text_short = text[...].astype(BF16)
    image_inv = inverse_norm(image[...])
    norms[...] = jnp.broadcast_to(image_inv, norms.shape)
    image[...] = image[...] * image_inv
    image_short = image[...].astype(BF16)
    scale = jnp.exp(jnp.full((1, 1), log_scale[0], F32))
    logits = scale * lax.dot_general(
        image_short, text_short, ROWWISE, preferred_element_type=F32
    )
    row_max = jnp.max(logits, axis=1, keepdims=True)
    row_lse = row_max + jnp.log(jnp.sum(jnp.exp(logits - row_max), axis=1, keepdims=True))
    col_max = jnp.max(logits, axis=0, keepdims=True)
    col_lse = col_max + jnp.log(jnp.sum(jnp.exp(logits - col_max), axis=0, keepdims=True))
    eye = (
        lax.broadcasted_iota(jnp.int32, logits.shape, 0)
        == lax.broadcasted_iota(jnp.int32, logits.shape, 1)
    ).astype(F32)
    coef = factor * (jnp.exp(logits - row_lse) + jnp.exp(logits - col_lse) - 2.0 * eye)
    loss = factor * (
        jnp.sum(row_lse, axis=0, keepdims=True)
        + jnp.sum(col_lse, axis=1, keepdims=True)
        - 2.0 * jnp.sum(jnp.sum(eye * logits, axis=1, keepdims=True), axis=0, keepdims=True)
    )
    scale_grad = jnp.sum(jnp.sum(coef * logits, axis=1, keepdims=True), axis=0, keepdims=True)
    coefs[...] = coef
    own = pl.multiple_of((z * 2 + core) * rows, 8)
    grad_unit = scale * jnp.dot(
        coefs[pl.ds(own, rows), :].astype(BF16), text_short, preferred_element_type=F32
    )
    unit = image[pl.ds(own, rows), :]
    grads[0] = (
        (grad_unit - unit * jnp.sum(unit * grad_unit, axis=-1, keepdims=True))
        * norms[pl.ds(own, rows), :1]
    ).astype(BF16)
    grad_unit = scale * jnp.dot(coef.T.astype(BF16), image_short, preferred_element_type=F32)
    unit = text[...]
    grad_all[...] = (
        grad_unit - unit * jnp.sum(unit * grad_unit, axis=-1, keepdims=True)
    ) * text_inv
    grads[1] = grad_all[pl.ds(own, rows), :].astype(BF16)
    for side in range(2):
        grad_cols[side] = grad_all[:, side * half : (side + 1) * half].astype(BF16)
    share[...] = jnp.dot(
        hidden_t[pl.ds(pl.multiple_of(z * 2 * depth, 8), 2 * depth), :].astype(BF16),
        grad_cols[core],
        preferred_element_type=F32,
    )
    totals = lanes_of(in_parts(loss) + in_parts(scale_grad), 2 * y + x, (16, half))
    keep[:depth, :] = share[pl.ds(pl.multiple_of(x * depth, 8), depth), :].astype(BF16)
    keep[depth:, :] = totals.astype(BF16)
    send[:depth, :] = share[pl.ds(pl.multiple_of((1 - x) * depth, 8), depth), :].astype(BF16)
    send[depth:, :] = totals.astype(BF16)


def on_device_whole_group(image_embed, text_hidden, text_rest, proj_window, log_scale):
    rows, width = image_embed.shape[1:]
    depth = proj_window.shape[0]
    total_rows, total_depth, half = rows * 8, depth * 8, width // 2
    factor = 1.0 / (2.0 * total_rows * lax.axis_size("rep"))
    z, x, y, core = own_place()
    ahead = is_ahead(x, core)
    own = lax.dynamic_slice_in_dim(proj_window, core * half, half, 1)
    own, = lax.optimization_barrier((own,))
    samples = jnp.concatenate([image_embed[0], text_rest[0], text_hidden[0]], axis=1)
    far = z_far(own)
    even = jnp.stack([own, far])
    first = first_move(samples)
    own_rows = jnp.where(ahead, samples, first)
    near = z_near(own)[None]
    (tied_second_0,), _ = lax.optimization_barrier(((own_rows,), far))
    second = second_move(tied_second_0)
    last = z_near(far)[None]
    even_x = x_peer(even)
    third = z_near(first)
    (tied_odd_x_0, tied_odd_x_1,), _ = lax.optimization_barrier(((near, last,), first))
    odd_x = x_peer(jnp.concatenate([tied_odd_x_0, tied_odd_x_1]))
    fourth = fourth_move(second)
    fourth_rows = jnp.where(ahead, first, fourth)
    (tied_cg0_0, tied_cg0_1,), _ = lax.optimization_barrier(((own_rows, second,), odd_x))
    cg0 = core_peer(jnp.stack([tied_cg0_0, tied_cg0_1]))
    cg1 = core_peer(third)
    cg2 = core_peer(fourth_rows)
    cq0 = core_peer(jnp.concatenate([even, near, last, even_x]))
    (tied_cq1_0,), _ = lax.optimization_barrier(((odd_x,), third))
    cq1 = core_peer(tied_cq1_0)
    rows_here = (own_rows, second, third, fourth_rows)
    rows_there = (cg0[0], cg0[1], cg1, cg2)
    proj_here = (even, near, last, even_x, odd_x)
    proj_there = (cq0[0:2], cq0[2:3], cq0[3:4], cq0[4:6], cq1)
    arrived = rows_here + rows_there + proj_here + proj_there
    keep, send, grads = pl.pallas_call(
        functools.partial(group_kernel, factor),
        out_shape=(
            jax.ShapeDtypeStruct((depth + 16, half), BF16),
            jax.ShapeDtypeStruct((depth + 16, half), BF16),
            jax.ShapeDtypeStruct((2, rows, width), BF16),
        ),
        in_specs=[IN_SMEM] + [IN_VMEM] * len(arrived),
        out_specs=[IN_VMEM] * 3,
        scratch_shapes=[
            pltpu.VMEM((total_rows, width), F32),
            pltpu.VMEM((total_rows, width), F32),
            pltpu.VMEM((total_rows, total_depth), F32),
            pltpu.VMEM((total_depth, total_rows), F32),
            pltpu.VMEM((total_rows, 128), F32),
            pltpu.VMEM((2, total_depth, half), BF16),
            pltpu.VMEM((total_rows, total_rows), F32),
            pltpu.VMEM((total_rows, width), F32),
            pltpu.VMEM((2, total_rows, half), BF16),
            pltpu.VMEM((2 * depth, half), F32),
        ],
        compiler_params=pltpu.CompilerParams(vmem_limit_bytes=40 * 2**20),
        name="group_kernel",
    )(
        log_scale,
        *arrived
    )
    over_y, over_x, over_both = y_peer(keep), x_peer(send), xy_peer(send)
    (tied_grads,), _ = lax.optimization_barrier(((grads,), over_y))
    grads = jnp.where(ahead, grads, trade_back(tied_grads))
    image_out, text_out = grads[0][None], grads[1][None]
    share = (keep.astype(F32) + over_y.astype(F32)) + (over_x.astype(F32) + over_both.astype(F32))
    ours = share[:depth]
    theirs = core_peer(ours)
    grad_proj = jnp.where(
        core == 0,
        jnp.concatenate([ours, theirs], axis=1),
        jnp.concatenate([theirs, ours], axis=1),
    )
    totals = jnp.sum(share[depth, :24].reshape(2, 12), axis=1)
    return totals[0:1], totals[1:2], image_out, text_out, grad_proj


def solution(mesh):
    sizes = dict(mesh.shape)
    whole_group = sizes["blk"] == 8 and sizes["rep"] == 4
    return jax.shard_map(
        on_device_whole_group if whole_group else on_device,
        mesh=mesh,
        in_specs=(
            P("rep", "blk", None),
            P("rep", "blk", None),
            P("rep", "blk", None),
            P("blk", None),
            P(),
        ),
        out_specs=(P(), P(), P("rep", "blk", None), P("rep", "blk", None), P("blk", None)),
        check_vma=False,
    )
```

```python
import functools

import jax
import jax.numpy as jnp
from jax import lax
from jax.experimental import pallas as pl
from jax.experimental.pallas import tpu as pltpu
from jax.sharding import PartitionSpec as P


def joined(value, axis, join):
    pieces = jax.tree.map(lambda part: lax.all_gather(part, axis), value)
    head = jax.tree.map(lambda part: part[0], pieces)
    tail = jax.tree.map(lambda part: part[1:], pieces)
    running, _ = lax.scan(lambda running, slab: (join(running, slab), None), head, tail)
    return running


def unit_rows(values):
    row_norm = jnp.sqrt(jnp.sum(values * values, axis=-1, keepdims=True) + 1e-06)
    return (values / row_norm, row_norm)


def unit_back(unit_vec, row_norm, grad_unit):
    return (grad_unit - unit_vec * jnp.sum(unit_vec * grad_unit, axis=-1, keepdims=True)) / row_norm


def pair_products(left, right):
    return lax.dot_general(
        left, right, (((1,), (1,)), ((), ())), preferred_element_type=jnp.float32
    )


def combine_parts(earlier, later):
    col_top = jnp.maximum(earlier[0], later[0])
    return (
        col_top,
        earlier[1] * jnp.exp(earlier[0] - col_top) + later[1] * jnp.exp(later[0] - col_top),
    )


def on_device(image_embed, text_hidden, text_rest, proj_window, log_scale):
    hidden = text_hidden[0]
    local_rows = hidden.shape[0]
    group_rows = local_rows * lax.axis_size("blk")
    offset = lax.axis_index("blk") * local_rows
    factor = 1.0 / (2.0 * group_rows * lax.axis_size("rep"))
    logit_scale = jnp.exp(log_scale[0])
    columns = hidden
    projected = jnp.dot(
        columns,
        lax.all_gather(proj_window, "blk", axis=0, tiled=True),
        preferred_element_type=jnp.float32,
    )
    text_unit, text_norm = unit_rows(text_rest[0].astype(jnp.float32) + projected)
    image_unit, image_norm = unit_rows(image_embed[0].astype(jnp.float32))
    text_short = text_unit.astype(jnp.bfloat16)
    image_short = image_unit.astype(jnp.bfloat16)
    all_text = lax.all_gather(text_short, "blk", axis=0, tiled=True)
    logits = logit_scale * pair_products(image_short, all_text)
    row_lse = jax.nn.logsumexp(logits, axis=1)
    col_max = jnp.max(logits, axis=0)
    col_sum = jnp.sum(jnp.exp(logits - col_max[None, :]), axis=0)
    col_top, col_total = joined((col_max, col_sum), "blk", combine_parts)
    col_lse = col_top + jnp.log(col_total)
    positions = lax.broadcasted_iota(jnp.int32, (local_rows, group_rows), 1)
    own_rows = lax.broadcasted_iota(jnp.int32, (local_rows, group_rows), 0) + offset
    diagonal_mask = (positions == own_rows).astype(jnp.float32)
    own_col = lax.dynamic_slice_in_dim(col_lse, offset, local_rows, 0)
    loss_local = factor * (
        jnp.sum(row_lse) + jnp.sum(own_col) - 2.0 * jnp.sum(diagonal_mask * logits)
    )
    coef_image = factor * (
        jnp.exp(logits - row_lse[:, None])
        + jnp.exp(logits - col_lse[None, :])
        - 2.0 * diagonal_mask
    )
    scale_local = jnp.sum(coef_image * logits)
    grad_image_unit = logit_scale * jnp.dot(
        coef_image.astype(jnp.bfloat16), all_text, preferred_element_type=jnp.float32
    )
    grad_image = unit_back(image_unit, image_norm, grad_image_unit).astype(jnp.bfloat16)
    row_all = lax.all_gather(row_lse, "blk", axis=0, tiled=True)
    all_image = lax.all_gather(image_short, "blk", axis=0, tiled=True)
    cross_logits = logit_scale * pair_products(text_short, all_image)
    coef_text = factor * (
        jnp.exp(cross_logits - row_all[None, :])
        + jnp.exp(cross_logits - own_col[:, None])
        - 2.0 * diagonal_mask
    )
    grad_text_unit = logit_scale * jnp.dot(
        coef_text.astype(jnp.bfloat16), all_image, preferred_element_type=jnp.float32
    )
    grad_text = unit_back(text_unit, text_norm, grad_text_unit).astype(jnp.bfloat16)
    columns = hidden
    grad_share = lax.psum_scatter(
        lax.dot_general(
            columns, grad_text, (((0,), (0,)), ((), ())), preferred_element_type=jnp.float32
        ),
        "blk",
        scatter_dimension=0,
        tiled=True,
    )
    grad_proj = lax.psum(grad_share, "rep")
    loss_value, scale_grad = lax.psum((loss_local, scale_local), ("blk", "rep"))
    return (
        loss_value.reshape(1),
        scale_grad.reshape(1),
        grad_image[None],
        grad_text[None],
        grad_proj,
    )


F32 = jnp.float32
BF16 = jnp.bfloat16
ROWWISE = (((1,), (1,)), ((), ()))
IN_VMEM = pl.BlockSpec(memory_space=pltpu.VMEM)
IN_SMEM = pl.BlockSpec(memory_space=pltpu.SMEM)
ROW_STEPS = ((0, 1, 3, 2), (0, 2, 1, 3))
PROJ_STEPS = (((0, 2), 0), ((1,), 0), ((3,), 0), ((0, 2), 1), ((1, 3), 1))

def number(z, x, y, core):
    return (z * 2 + x) * 4 + y * 2 + core


def after(done, *values):
    return lax.optimization_barrier((values, done))[0]


def own_place():
    blk, rep = lax.axis_index("blk"), lax.axis_index("rep")
    return blk // 2, blk % 2, rep // 2, rep % 2


def moved(value, to):
    places = [(z, x, y, core) for z in range(4) for x in range(2) for y in range(2) for core in range(2)]
    return lax.ppermute(
        value, ("blk", "rep"), [(number(*place), number(*to(*place))) for place in places]
    )


def z_near(value):
    return moved(value, lambda z, x, y, core: (z ^ 1, x, y, core))


def z_far(value):
    return moved(value, lambda z, x, y, core: (z ^ 2, x, y, core))


def x_peer(value):
    return moved(value, lambda z, x, y, core: (z, 1 - x, y, core))


def y_peer(value):
    return moved(value, lambda z, x, y, core: (z, x, 1 - y, core))


def xy_peer(value):
    return moved(value, lambda z, x, y, core: (z, 1 - x, 1 - y, core))


def core_peer(value):
    return moved(value, lambda z, x, y, core: (z, x, y, 1 - core))


def is_ahead(x, core):
    return x == core


def trade(z, x, y, core):
    return z, core, y, x


def first_move(value):
    return moved(value, lambda z, x, y, core: (z ^ 2, x, y, core) if is_ahead(x, core) else trade(z, x, y, core))


def second_move(value):
    return moved(value, lambda z, x, y, core: (z ^ 1 if is_ahead(x, core) else z ^ 2, x, y, core))


def fourth_move(value):
    return moved(value, lambda z, x, y, core: (z, 1 - x, y, 1 - core) if is_ahead(x, core) else (z ^ 1, x, y, core))


def trade_back(value):
    return moved(value, lambda z, x, y, core: (z ^ 1, x, y, core) if is_ahead(x, core) else trade(z, x, y, core))


def in_parts(value):
    high = value.astype(BF16)
    rest = value - high.astype(F32)
    middle = rest.astype(BF16)
    return high, middle, (rest - middle.astype(F32)).astype(BF16)


def lanes_of(values, group, shape):
    lane = lax.broadcasted_iota(jnp.int32, shape, 1)
    row = jnp.zeros(shape, F32)
    for at, value in enumerate(values):
        row = jnp.where(lane == at * 4 + group, value.astype(F32), row)
    return row


def inverse_norm(values):
    return lax.rsqrt(jnp.sum(values * values, axis=-1, keepdims=True) + 1e-06)


def group_kernel(factor, log_scale, *refs):
    count = 2 * len(PROJ_STEPS)
    rows_here, rows_there, projs = refs[:4], refs[4:8], refs[8 : 8 + count]
    keep, send, grads = refs[8 + count : 11 + count]
    image, text, hidden, hidden_t, norms, proj, coefs, grad_all, share = refs[11 + count :]
    z, x, y, core = own_place()
    rows, depth = rows_here[0].shape[0], proj.shape[1] // 8
    width = image.shape[1]
    half = width // 2
    ahead = is_ahead(x, core)
    for side, blocks in enumerate((rows_here, rows_there)):
        for block, *steps in zip(blocks, *ROW_STEPS):
            step = jnp.where(ahead, steps[side], steps[1 - side])
            start = pl.multiple_of(((z ^ step) * 2 + (core ^ side)) * rows, 8)
            image[pl.ds(start, rows), :] = block[:, :width].astype(F32)
            text[pl.ds(start, rows), :] = block[:, width : 2 * width].astype(F32)
            hidden[pl.ds(start, rows), :] = block[:, 2 * width :].astype(F32)
    for at, blocks in enumerate(projs):
        side, kind = divmod(at, len(PROJ_STEPS))
        steps, column = PROJ_STEPS[kind]
        for block, step in enumerate(steps):
            start = pl.multiple_of(((z ^ step) * 2 + (x ^ column)) * depth, 16)
            proj[core ^ side, pl.ds(start, depth), :] = blocks[block]
    hidden_short = hidden[...].astype(BF16)
    for side in range(2):
        text[:, side * half : (side + 1) * half] += jnp.dot(
            hidden_short, proj[side], preferred_element_type=F32
        )
    hidden_t[...] = hidden[...].T
    text_inv = inverse_norm(text[...])
    text_short = (text[...] * text_inv).astype(BF16)
    image_inv = inverse_norm(image[...])
    norms[...] = jnp.broadcast_to(image_inv, norms.shape)
    image_short = (image[...] * image_inv).astype(BF16)
    scale = jnp.exp(jnp.full((1, 1), log_scale[0], F32))
    logits = scale * lax.dot_general(
        image_short, text_short, ROWWISE, preferred_element_type=F32
    )
    row_max = jnp.max(logits, axis=1, keepdims=True)
    row_lse = row_max + jnp.log(jnp.sum(jnp.exp(logits - row_max), axis=1, keepdims=True))
    col_max = jnp.max(logits, axis=0, keepdims=True)
    col_lse = col_max + jnp.log(jnp.sum(jnp.exp(logits - col_max), axis=0, keepdims=True))
    eye = (
        lax.broadcasted_iota(jnp.int32, logits.shape, 0)
        == lax.broadcasted_iota(jnp.int32, logits.shape, 1)
    ).astype(F32)
    coef = factor * (jnp.exp(logits - row_lse) + jnp.exp(logits - col_lse) - 2.0 * eye)
    loss = factor * (
        jnp.sum(row_lse, axis=0, keepdims=True)
        + jnp.sum(col_lse, axis=1, keepdims=True)
        - 2.0 * jnp.sum(jnp.sum(eye * logits, axis=1, keepdims=True), axis=0, keepdims=True)
    )
    scale_grad = jnp.sum(jnp.sum(coef * logits, axis=1, keepdims=True), axis=0, keepdims=True)
    coefs[...] = coef
    own = pl.multiple_of((z * 2 + core) * rows, 8)
    grad_unit = scale * jnp.dot(
        coefs[pl.ds(own, rows), :].astype(BF16), text_short, preferred_element_type=F32
    )
    inverse = norms[pl.ds(own, rows), :1]
    unit = image[pl.ds(own, rows), :] * inverse
    grads[0] = (
        (grad_unit - unit * jnp.sum(unit * grad_unit, axis=-1, keepdims=True)) * inverse
    ).astype(BF16)
    grad_unit = scale * jnp.dot(coef.T.astype(BF16), image_short, preferred_element_type=F32)
    unit = text[...] * text_inv
    grad_all[...] = (
        grad_unit - unit * jnp.sum(unit * grad_unit, axis=-1, keepdims=True)
    ) * text_inv
    grads[1] = grad_all[pl.ds(own, rows), :].astype(BF16)
    share[...] = jnp.dot(
        hidden_t[pl.ds(pl.multiple_of(z * 2 * depth, 8), 2 * depth), :].astype(BF16),
        grad_all[:, pl.ds(pl.multiple_of(core * half, 128), half)].astype(BF16),
        preferred_element_type=F32,
    )
    totals = lanes_of(in_parts(loss) + in_parts(scale_grad), 2 * y + x, (8, half))
    keep[:depth, :] = share[pl.ds(pl.multiple_of(x * depth, 8), depth), :].astype(BF16)
    keep[depth:, :] = totals.astype(BF16)
    send[:depth, :] = share[pl.ds(pl.multiple_of((1 - x) * depth, 8), depth), :].astype(BF16)
    send[depth:, :] = totals.astype(BF16)


def on_device_whole_group(image_embed, text_hidden, text_rest, proj_window, log_scale):
    rows, width = image_embed.shape[1:]
    depth = proj_window.shape[0]
    total_rows, total_depth, half = rows * 8, depth * 8, width // 2
    factor = 1.0 / (2.0 * total_rows * lax.axis_size("rep"))
    z, x, y, core = own_place()
    ahead = is_ahead(x, core)
    (own,) = lax.optimization_barrier((lax.dynamic_slice_in_dim(proj_window, core * half, half, 1),))
    samples = jnp.concatenate([image_embed[0], text_rest[0], text_hidden[0]], axis=1)
    far = z_far(own)
    even = jnp.stack([own, far])
    first = first_move(samples)
    own_rows = jnp.where(ahead, samples, first)
    near = z_near(own)[None]
    second = second_move(*after(far, own_rows))
    last = z_near(far)[None]
    even_x = x_peer(*after(near, even))
    third = z_near(first)
    odd_x = x_peer(jnp.concatenate([near, last]))
    fourth = jnp.where(ahead, first, fourth_move(second))
    there_01 = core_peer(jnp.stack(after(odd_x, own_rows, second)))
    there_third = core_peer(third)
    there_fourth = core_peer(fourth)
    proj_early = core_peer(jnp.concatenate([even, near, last, even_x]))
    proj_late = core_peer(*after(third, odd_x))
    rows_here = own_rows, second, third, fourth
    rows_there = there_01[0], there_01[1], there_third, there_fourth
    proj_here = even, near, last, even_x, odd_x
    proj_there = proj_early[0:2], proj_early[2:3], proj_early[3:4], proj_early[4:6], proj_late
    arrived = rows_here + rows_there + proj_here + proj_there
    keep, send, grads = pl.pallas_call(
        functools.partial(group_kernel, factor),
        out_shape=(
            jax.ShapeDtypeStruct((depth + 8, half), BF16),
            jax.ShapeDtypeStruct((depth + 8, half), BF16),
            jax.ShapeDtypeStruct((2, rows, width), BF16),
        ),
        in_specs=[IN_SMEM] + [IN_VMEM] * len(arrived),
        out_specs=[IN_VMEM] * 3,
        scratch_shapes=[
            pltpu.VMEM((total_rows, width), F32),
            pltpu.VMEM((total_rows, width), F32),
            pltpu.VMEM((total_rows, total_depth), F32),
            pltpu.VMEM((total_depth, total_rows), F32),
            pltpu.VMEM((total_rows, 128), F32),
            pltpu.VMEM((2, total_depth, half), BF16),
            pltpu.VMEM((total_rows, total_rows), F32),
            pltpu.VMEM((total_rows, width), F32),
            pltpu.VMEM((2 * depth, half), F32),
        ],
        compiler_params=pltpu.CompilerParams(vmem_limit_bytes=40 * 2**20),
        name="group_kernel",
    )(
        log_scale,
        *arrived
    )
    over_y, over_x, over_both = y_peer(keep), x_peer(send), xy_peer(send)
    grads = jnp.where(ahead, grads, trade_back(*after(over_y, grads)))
    share = (keep.astype(F32) + over_y.astype(F32)) + (over_x.astype(F32) + over_both.astype(F32))
    ours = share[:depth]
    theirs = core_peer(ours)
    grad_proj = jnp.where(
        core == 0,
        jnp.concatenate([ours, theirs], axis=1),
        jnp.concatenate([theirs, ours], axis=1),
    )
    totals = jnp.sum(share[depth, :24].reshape(2, 12), axis=1)
    return totals[0:1], totals[1:2], grads[0][None], grads[1][None], grad_proj


def solution(mesh):
    sizes = dict(mesh.shape)
    whole_group = sizes["blk"] == 8 and sizes["rep"] == 4
    return jax.shard_map(
        on_device_whole_group if whole_group else on_device,
        mesh=mesh,
        in_specs=(
            P("rep", "blk", None),
            P("rep", "blk", None),
            P("rep", "blk", None),
            P("blk", None),
            P(),
        ),
        out_specs=(P(), P(), P("rep", "blk", None), P("rep", "blk", None), P("blk", None)),
        check_vma=False,
    )
```

```python
import functools

import jax
import jax.numpy as jnp
from jax import lax
from jax.experimental import pallas as pl
from jax.experimental.pallas import tpu as pltpu
from jax.sharding import PartitionSpec as P


def joined(value, axis, join):
    pieces = jax.tree.map(lambda part: lax.all_gather(part, axis), value)
    head = jax.tree.map(lambda part: part[0], pieces)
    tail = jax.tree.map(lambda part: part[1:], pieces)
    running, _ = lax.scan(lambda running, slab: (join(running, slab), None), head, tail)
    return running


def unit_rows(values):
    row_norm = jnp.sqrt(jnp.sum(values * values, axis=-1, keepdims=True) + 1e-06)
    return (values / row_norm, row_norm)


def unit_back(unit_vec, row_norm, grad_unit):
    return (grad_unit - unit_vec * jnp.sum(unit_vec * grad_unit, axis=-1, keepdims=True)) / row_norm


def pair_products(left, right):
    return lax.dot_general(
        left, right, (((1,), (1,)), ((), ())), preferred_element_type=jnp.float32
    )


def combine_parts(earlier, later):
    col_top = jnp.maximum(earlier[0], later[0])
    return (
        col_top,
        earlier[1] * jnp.exp(earlier[0] - col_top) + later[1] * jnp.exp(later[0] - col_top),
    )


def on_device(image_embed, text_hidden, text_rest, proj_window, log_scale):
    hidden = text_hidden[0]
    local_rows = hidden.shape[0]
    group_rows = local_rows * lax.axis_size("blk")
    offset = lax.axis_index("blk") * local_rows
    factor = 1.0 / (2.0 * group_rows * lax.axis_size("rep"))
    logit_scale = jnp.exp(log_scale[0])
    columns = hidden
    projected = jnp.dot(
        columns,
        lax.all_gather(proj_window, "blk", axis=0, tiled=True),
        preferred_element_type=jnp.float32,
    )
    text_unit, text_norm = unit_rows(text_rest[0].astype(jnp.float32) + projected)
    image_unit, image_norm = unit_rows(image_embed[0].astype(jnp.float32))
    text_short = text_unit.astype(jnp.bfloat16)
    image_short = image_unit.astype(jnp.bfloat16)
    all_text = lax.all_gather(text_short, "blk", axis=0, tiled=True)
    logits = logit_scale * pair_products(image_short, all_text)
    row_lse = jax.nn.logsumexp(logits, axis=1)
    col_max = jnp.max(logits, axis=0)
    col_sum = jnp.sum(jnp.exp(logits - col_max[None, :]), axis=0)
    col_top, col_total = joined((col_max, col_sum), "blk", combine_parts)
    col_lse = col_top + jnp.log(col_total)
    positions = lax.broadcasted_iota(jnp.int32, (local_rows, group_rows), 1)
    own_rows = lax.broadcasted_iota(jnp.int32, (local_rows, group_rows), 0) + offset
    diagonal_mask = (positions == own_rows).astype(jnp.float32)
    own_col = lax.dynamic_slice_in_dim(col_lse, offset, local_rows, 0)
    loss_local = factor * (
        jnp.sum(row_lse) + jnp.sum(own_col) - 2.0 * jnp.sum(diagonal_mask * logits)
    )
    coef_image = factor * (
        jnp.exp(logits - row_lse[:, None])
        + jnp.exp(logits - col_lse[None, :])
        - 2.0 * diagonal_mask
    )
    scale_local = jnp.sum(coef_image * logits)
    grad_image_unit = logit_scale * jnp.dot(
        coef_image.astype(jnp.bfloat16), all_text, preferred_element_type=jnp.float32
    )
    grad_image = unit_back(image_unit, image_norm, grad_image_unit).astype(jnp.bfloat16)
    row_all = lax.all_gather(row_lse, "blk", axis=0, tiled=True)
    all_image = lax.all_gather(image_short, "blk", axis=0, tiled=True)
    cross_logits = logit_scale * pair_products(text_short, all_image)
    coef_text = factor * (
        jnp.exp(cross_logits - row_all[None, :])
        + jnp.exp(cross_logits - own_col[:, None])
        - 2.0 * diagonal_mask
    )
    grad_text_unit = logit_scale * jnp.dot(
        coef_text.astype(jnp.bfloat16), all_image, preferred_element_type=jnp.float32
    )
    grad_text = unit_back(text_unit, text_norm, grad_text_unit).astype(jnp.bfloat16)
    columns = hidden
    grad_share = lax.psum_scatter(
        lax.dot_general(
            columns, grad_text, (((0,), (0,)), ((), ())), preferred_element_type=jnp.float32
        ),
        "blk",
        scatter_dimension=0,
        tiled=True,
    )
    grad_proj = lax.psum(grad_share, "rep")
    loss_value, scale_grad = lax.psum((loss_local, scale_local), ("blk", "rep"))
    return (
        loss_value.reshape(1),
        scale_grad.reshape(1),
        grad_image[None],
        grad_text[None],
        grad_proj,
    )


F32 = jnp.float32
BF16 = jnp.bfloat16
ROWWISE = (((1,), (1,)), ((), ()))
IN_VMEM = pl.BlockSpec(memory_space=pltpu.VMEM)
IN_SMEM = pl.BlockSpec(memory_space=pltpu.SMEM)
ROW_STEPS = ((0, 1, 3, 2), (0, 2, 1, 3))
PROJ_STEPS = (((0, 2), 0), ((1,), 0), ((3,), 0), ((0, 2), 1), ((1, 3), 1))

def number(z, x, y, core):
    return (z * 2 + x) * 4 + y * 2 + core


def after(done, *values):
    return lax.optimization_barrier((values, done))[0]


def own_place():
    blk, rep = lax.axis_index("blk"), lax.axis_index("rep")
    return blk // 2, blk % 2, rep // 2, rep % 2


def moved(value, to):
    places = [(z, x, y, core) for z in range(4) for x in range(2) for y in range(2) for core in range(2)]
    return lax.ppermute(
        value, ("blk", "rep"), [(number(*place), number(*to(*place))) for place in places]
    )


def z_near(value):
    return moved(value, lambda z, x, y, core: (z ^ 1, x, y, core))


def z_far(value):
    return moved(value, lambda z, x, y, core: (z ^ 2, x, y, core))


def x_peer(value):
    return moved(value, lambda z, x, y, core: (z, 1 - x, y, core))


def y_peer(value):
    return moved(value, lambda z, x, y, core: (z, x, 1 - y, core))


def xy_peer(value):
    return moved(value, lambda z, x, y, core: (z, 1 - x, 1 - y, core))


def core_peer(value):
    return moved(value, lambda z, x, y, core: (z, x, y, 1 - core))


def is_ahead(x, core):
    return x == core


def trade(z, x, y, core):
    return z, core, y, x


def first_move(value):
    return moved(value, lambda z, x, y, core: (z ^ 2, x, y, core) if is_ahead(x, core) else trade(z, x, y, core))


def second_move(value):
    return moved(value, lambda z, x, y, core: (z ^ 1 if is_ahead(x, core) else z ^ 2, x, y, core))


def fourth_move(value):
    return moved(value, lambda z, x, y, core: (z, 1 - x, y, 1 - core) if is_ahead(x, core) else (z ^ 1, x, y, core))


def trade_back(value):
    return moved(value, lambda z, x, y, core: (z ^ 1, x, y, core) if is_ahead(x, core) else trade(z, x, y, core))


def in_parts(value):
    high = value.astype(BF16)
    rest = value - high.astype(F32)
    middle = rest.astype(BF16)
    return high, middle, (rest - middle.astype(F32)).astype(BF16)


def lanes_of(values, group, shape):
    lane = lax.broadcasted_iota(jnp.int32, shape, 1)
    row = jnp.zeros(shape, F32)
    for at, value in enumerate(values):
        row = jnp.where(lane == at * 4 + group, value.astype(F32), row)
    return row


def inverse_norm(values):
    return lax.rsqrt(jnp.sum(values * values, axis=-1, keepdims=True) + 1e-06)


def group_kernel(factor, log_scale, *refs):
    count = 2 * len(PROJ_STEPS)
    rows_here, rows_there, projs = refs[:4], refs[4:8], refs[8 : 8 + count]
    keep, send, grads = refs[8 + count : 11 + count]
    image, text, hidden, hidden_t, norms, proj, coefs, grad_all, share = refs[11 + count :]
    z, x, y, core = own_place()
    rows, depth = rows_here[0].shape[0], proj.shape[1] // 8
    width = image.shape[1]
    half = width // 2
    ahead = is_ahead(x, core)
    for side, blocks in enumerate((rows_here, rows_there)):
        for block, *steps in zip(blocks, *ROW_STEPS):
            step = jnp.where(ahead, steps[side], steps[1 - side])
            start = pl.multiple_of(((z ^ step) * 2 + (core ^ side)) * rows, 8)
            image[pl.ds(start, rows), :] = block[:, :width].astype(F32)
            text[pl.ds(start, rows), :] = block[:, width : 2 * width].astype(F32)
            hidden[pl.ds(start, rows), :] = block[:, 2 * width :].astype(F32)
    for at, blocks in enumerate(projs):
        side, kind = divmod(at, len(PROJ_STEPS))
        steps, column = PROJ_STEPS[kind]
        for block, step in enumerate(steps):
            start = pl.multiple_of(((z ^ step) * 2 + (x ^ column)) * depth, 16)
            proj[core ^ side, pl.ds(start, depth), :] = blocks[block]
    hidden_short = hidden[...].astype(BF16)
    for side in range(2):
        text[:, side * half : (side + 1) * half] += jnp.dot(
            hidden_short, proj[side], preferred_element_type=F32
        )
    hidden_t[...] = hidden[...].T
    text_inv = inverse_norm(text[...])
    text_short = (text[...] * text_inv).astype(BF16)
    image_inv = inverse_norm(image[...])
    norms[...] = jnp.broadcast_to(image_inv, norms.shape)
    image_short = (image[...] * image_inv).astype(BF16)
    scale = jnp.exp(jnp.full((1, 1), log_scale[0], F32))
    logits = scale * lax.dot_general(
        image_short, text_short, ROWWISE, preferred_element_type=F32
    )
    row_max = jnp.max(logits, axis=1, keepdims=True)
    row_lse = row_max + jnp.log(jnp.sum(jnp.exp(logits - row_max), axis=1, keepdims=True))
    col_max = jnp.max(logits, axis=0, keepdims=True)
    col_lse = col_max + jnp.log(jnp.sum(jnp.exp(logits - col_max), axis=0, keepdims=True))
    eye = (
        lax.broadcasted_iota(jnp.int32, logits.shape, 0)
        == lax.broadcasted_iota(jnp.int32, logits.shape, 1)
    ).astype(F32)
    coef = factor * (jnp.exp(logits - row_lse) + jnp.exp(logits - col_lse) - 2.0 * eye)
    loss = factor * (
        jnp.sum(row_lse, axis=0, keepdims=True)
        + jnp.sum(col_lse, axis=1, keepdims=True)
        - 2.0 * jnp.sum(jnp.sum(eye * logits, axis=1, keepdims=True), axis=0, keepdims=True)
    )
    scale_grad = jnp.sum(jnp.sum(coef * logits, axis=1, keepdims=True), axis=0, keepdims=True)
    coefs[...] = coef
    own = pl.multiple_of((z * 2 + core) * rows, 8)
    grad_unit = scale * jnp.dot(
        coefs[pl.ds(own, rows), :].astype(BF16), text_short, preferred_element_type=F32
    )
    inverse = norms[pl.ds(own, rows), :1]
    unit = image[pl.ds(own, rows), :] * inverse
    grads[0] = (
        (grad_unit - unit * jnp.sum(unit * grad_unit, axis=-1, keepdims=True)) * inverse
    ).astype(BF16)
    grad_unit = scale * jnp.dot(coef.T.astype(BF16), image_short, preferred_element_type=F32)
    unit = text[...] * text_inv
    grad_all[...] = (
        grad_unit - unit * jnp.sum(unit * grad_unit, axis=-1, keepdims=True)
    ) * text_inv
    grads[1] = grad_all[pl.ds(own, rows), :].astype(BF16)
    share[...] = jnp.dot(
        hidden_t[pl.ds(pl.multiple_of(z * 2 * depth, 8), 2 * depth), :].astype(BF16),
        grad_all[:, pl.ds(pl.multiple_of(core * half, 128), half)].astype(BF16),
        preferred_element_type=F32,
    )
    totals = lanes_of(in_parts(loss) + in_parts(scale_grad), 2 * y + x, (8, half))
    for part, at in ((keep, x), (send, 1 - x)):
        rows_of = share[pl.ds(pl.multiple_of(at * depth, 8), depth), :]
        part[...] = jnp.concatenate([rows_of, totals]).astype(BF16)


def on_device_whole_group(image_embed, text_hidden, text_rest, proj_window, log_scale):
    rows, width = image_embed.shape[1:]
    depth = proj_window.shape[0]
    total_rows, total_depth, half = rows * 8, depth * 8, width // 2
    factor = 1.0 / (2.0 * total_rows * lax.axis_size("rep"))
    z, x, y, core = own_place()
    ahead = is_ahead(x, core)
    (own,) = lax.optimization_barrier((lax.dynamic_slice_in_dim(proj_window, core * half, half, 1),))
    samples = jnp.concatenate([image_embed[0], text_rest[0], text_hidden[0]], axis=1)
    far = z_far(own)
    even = jnp.stack([own, far])
    first = first_move(samples)
    own_rows = jnp.where(ahead, samples, first)
    near = z_near(own)[None]
    second = second_move(*after(far, own_rows))
    last = z_near(far)[None]
    even_x = x_peer(*after(near, even))
    third = z_near(first)
    odd_x = x_peer(jnp.concatenate([near, last]))
    fourth = jnp.where(ahead, first, fourth_move(second))
    there_01 = core_peer(jnp.stack(after(odd_x, own_rows, second)))
    there_third = core_peer(third)
    there_fourth = core_peer(fourth)
    proj_early = core_peer(jnp.concatenate([even, near, last, even_x]))
    proj_late = core_peer(*after(third, odd_x))
    rows_here = own_rows, second, third, fourth
    rows_there = there_01[0], there_01[1], there_third, there_fourth
    proj_here = even, near, last, even_x, odd_x
    proj_there = proj_early[0:2], proj_early[2:3], proj_early[3:4], proj_early[4:6], proj_late
    arrived = rows_here + rows_there + proj_here + proj_there
    keep, send, grads = pl.pallas_call(
        functools.partial(group_kernel, factor),
        out_shape=(
            jax.ShapeDtypeStruct((depth + 8, half), BF16),
            jax.ShapeDtypeStruct((depth + 8, half), BF16),
            jax.ShapeDtypeStruct((2, rows, width), BF16),
        ),
        in_specs=[IN_SMEM] + [IN_VMEM] * len(arrived),
        out_specs=[IN_VMEM] * 3,
        scratch_shapes=[
            pltpu.VMEM((total_rows, width), F32),
            pltpu.VMEM((total_rows, width), F32),
            pltpu.VMEM((total_rows, total_depth), F32),
            pltpu.VMEM((total_depth, total_rows), F32),
            pltpu.VMEM((total_rows, 128), F32),
            pltpu.VMEM((2, total_depth, half), BF16),
            pltpu.VMEM((total_rows, total_rows), F32),
            pltpu.VMEM((total_rows, width), F32),
            pltpu.VMEM((2 * depth, half), F32),
        ],
        compiler_params=pltpu.CompilerParams(vmem_limit_bytes=40 * 2**20),
        name="group_kernel",
    )(
        log_scale,
        *arrived
    )
    over_y, over_x, over_both = y_peer(keep), x_peer(send), xy_peer(send)
    grads = jnp.where(ahead, grads, trade_back(grads))
    share = (keep.astype(F32) + over_y.astype(F32)) + (over_x.astype(F32) + over_both.astype(F32))
    ours = share[:depth]
    theirs = core_peer(ours)
    grad_proj = jnp.where(
        core == 0,
        jnp.concatenate([ours, theirs], axis=1),
        jnp.concatenate([theirs, ours], axis=1),
    )
    totals = jnp.sum(share[depth, :24].reshape(2, 12), axis=1)
    return totals[0:1], totals[1:2], grads[0][None], grads[1][None], grad_proj


def solution(mesh):
    sizes = dict(mesh.shape)
    whole_group = sizes["blk"] == 8 and sizes["rep"] == 4
    return jax.shard_map(
        on_device_whole_group if whole_group else on_device,
        mesh=mesh,
        in_specs=(
            P("rep", "blk", None),
            P("rep", "blk", None),
            P("rep", "blk", None),
            P("blk", None),
            P(),
        ),
        out_specs=(P(), P(), P("rep", "blk", None), P("rep", "blk", None), P("blk", None)),
        check_vma=False,
    )
```

```python
import functools

import jax
import jax.numpy as jnp
from jax import lax
from jax.experimental import pallas as pl
from jax.experimental.pallas import tpu as pltpu
from jax.sharding import PartitionSpec as P


def joined(value, axis, join):
    pieces = jax.tree.map(lambda part: lax.all_gather(part, axis), value)
    head = jax.tree.map(lambda part: part[0], pieces)
    tail = jax.tree.map(lambda part: part[1:], pieces)
    running, _ = lax.scan(lambda running, slab: (join(running, slab), None), head, tail)
    return running


def unit_rows(values):
    row_norm = jnp.sqrt(jnp.sum(values * values, axis=-1, keepdims=True) + 1e-06)
    return (values / row_norm, row_norm)


def unit_back(unit_vec, row_norm, grad_unit):
    return (grad_unit - unit_vec * jnp.sum(unit_vec * grad_unit, axis=-1, keepdims=True)) / row_norm


def pair_products(left, right):
    return lax.dot_general(
        left, right, (((1,), (1,)), ((), ())), preferred_element_type=jnp.float32
    )


def combine_parts(earlier, later):
    col_top = jnp.maximum(earlier[0], later[0])
    return (
        col_top,
        earlier[1] * jnp.exp(earlier[0] - col_top) + later[1] * jnp.exp(later[0] - col_top),
    )


def on_device(image_embed, text_hidden, text_rest, proj_window, log_scale):
    hidden = text_hidden[0]
    local_rows = hidden.shape[0]
    group_rows = local_rows * lax.axis_size("blk")
    offset = lax.axis_index("blk") * local_rows
    factor = 1.0 / (2.0 * group_rows * lax.axis_size("rep"))
    logit_scale = jnp.exp(log_scale[0])
    columns = hidden
    projected = jnp.dot(
        columns,
        lax.all_gather(proj_window, "blk", axis=0, tiled=True),
        preferred_element_type=jnp.float32,
    )
    text_unit, text_norm = unit_rows(text_rest[0].astype(jnp.float32) + projected)
    image_unit, image_norm = unit_rows(image_embed[0].astype(jnp.float32))
    text_short = text_unit.astype(jnp.bfloat16)
    image_short = image_unit.astype(jnp.bfloat16)
    all_text = lax.all_gather(text_short, "blk", axis=0, tiled=True)
    logits = logit_scale * pair_products(image_short, all_text)
    row_lse = jax.nn.logsumexp(logits, axis=1)
    col_max = jnp.max(logits, axis=0)
    col_sum = jnp.sum(jnp.exp(logits - col_max[None, :]), axis=0)
    col_top, col_total = joined((col_max, col_sum), "blk", combine_parts)
    col_lse = col_top + jnp.log(col_total)
    positions = lax.broadcasted_iota(jnp.int32, (local_rows, group_rows), 1)
    own_rows = lax.broadcasted_iota(jnp.int32, (local_rows, group_rows), 0) + offset
    diagonal_mask = (positions == own_rows).astype(jnp.float32)
    own_col = lax.dynamic_slice_in_dim(col_lse, offset, local_rows, 0)
    loss_local = factor * (
        jnp.sum(row_lse) + jnp.sum(own_col) - 2.0 * jnp.sum(diagonal_mask * logits)
    )
    coef_image = factor * (
        jnp.exp(logits - row_lse[:, None])
        + jnp.exp(logits - col_lse[None, :])
        - 2.0 * diagonal_mask
    )
    scale_local = jnp.sum(coef_image * logits)
    grad_image_unit = logit_scale * jnp.dot(
        coef_image.astype(jnp.bfloat16), all_text, preferred_element_type=jnp.float32
    )
    grad_image = unit_back(image_unit, image_norm, grad_image_unit).astype(jnp.bfloat16)
    row_all = lax.all_gather(row_lse, "blk", axis=0, tiled=True)
    all_image = lax.all_gather(image_short, "blk", axis=0, tiled=True)
    cross_logits = logit_scale * pair_products(text_short, all_image)
    coef_text = factor * (
        jnp.exp(cross_logits - row_all[None, :])
        + jnp.exp(cross_logits - own_col[:, None])
        - 2.0 * diagonal_mask
    )
    grad_text_unit = logit_scale * jnp.dot(
        coef_text.astype(jnp.bfloat16), all_image, preferred_element_type=jnp.float32
    )
    grad_text = unit_back(text_unit, text_norm, grad_text_unit).astype(jnp.bfloat16)
    columns = hidden
    grad_share = lax.psum_scatter(
        lax.dot_general(
            columns, grad_text, (((0,), (0,)), ((), ())), preferred_element_type=jnp.float32
        ),
        "blk",
        scatter_dimension=0,
        tiled=True,
    )
    grad_proj = lax.psum(grad_share, "rep")
    loss_value, scale_grad = lax.psum((loss_local, scale_local), ("blk", "rep"))
    return (
        loss_value.reshape(1),
        scale_grad.reshape(1),
        grad_image[None],
        grad_text[None],
        grad_proj,
    )


F32 = jnp.float32
BF16 = jnp.bfloat16
ROWWISE = (((1,), (1,)), ((), ()))
IN_VMEM = pl.BlockSpec(memory_space=pltpu.VMEM)
IN_SMEM = pl.BlockSpec(memory_space=pltpu.SMEM)
ROW_STEPS = ((0, 1, 3, 2), (0, 2, 1, 3))
PROJ_STEPS = (((0, 2), 0), ((1,), 0), ((3,), 0), ((0, 2), 1), ((1, 3), 1))

def number(z, x, y, core):
    return (z * 2 + x) * 4 + y * 2 + core


def after(done, *values):
    return lax.optimization_barrier((values, done))[0]


def own_place():
    blk, rep = lax.axis_index("blk"), lax.axis_index("rep")
    return blk // 2, blk % 2, rep // 2, rep % 2


def moved(value, to):
    places = [(z, x, y, core) for z in range(4) for x in range(2) for y in range(2) for core in range(2)]
    return lax.ppermute(
        value, ("blk", "rep"), [(number(*place), number(*to(*place))) for place in places]
    )


def z_near(value):
    return moved(value, lambda z, x, y, core: (z ^ 1, x, y, core))


def z_far(value):
    return moved(value, lambda z, x, y, core: (z ^ 2, x, y, core))


def x_peer(value):
    return moved(value, lambda z, x, y, core: (z, 1 - x, y, core))


def y_peer(value):
    return moved(value, lambda z, x, y, core: (z, x, 1 - y, core))


def xy_peer(value):
    return moved(value, lambda z, x, y, core: (z, 1 - x, 1 - y, core))


def core_peer(value):
    return moved(value, lambda z, x, y, core: (z, x, y, 1 - core))


def is_ahead(x, core):
    return x == core


def trade(z, x, y, core):
    return z, core, y, x


def first_move(value):
    return moved(value, lambda z, x, y, core: (z ^ 2, x, y, core) if is_ahead(x, core) else trade(z, x, y, core))


def second_move(value):
    return moved(value, lambda z, x, y, core: (z ^ 1 if is_ahead(x, core) else z ^ 2, x, y, core))


def fourth_move(value):
    return moved(value, lambda z, x, y, core: (z, 1 - x, y, 1 - core) if is_ahead(x, core) else (z ^ 1, x, y, core))


def trade_back(value):
    return moved(value, lambda z, x, y, core: (z ^ 1, x, y, core) if is_ahead(x, core) else trade(z, x, y, core))


def in_parts(value):
    high = value.astype(BF16)
    rest = value - high.astype(F32)
    middle = rest.astype(BF16)
    return high, middle, (rest - middle.astype(F32)).astype(BF16)


def lanes_of(values, group, shape):
    lane = lax.broadcasted_iota(jnp.int32, shape, 1)
    row = jnp.zeros(shape, F32)
    for at, value in enumerate(values):
        row = jnp.where(lane == at * 4 + group, value.astype(F32), row)
    return row


def inverse_norm(values):
    return lax.rsqrt(jnp.sum(values * values, axis=-1, keepdims=True) + 1e-06)


def group_kernel(factor, log_scale, *refs):
    count = 2 * len(PROJ_STEPS)
    rows_here, rows_there, projs = refs[:4], refs[4:8], refs[8 : 8 + count]
    keep, send, grads = refs[8 + count : 11 + count]
    image, text, hidden, hidden_t, norms, proj, coefs, grad_all, share = refs[11 + count :]
    z, x, y, core = own_place()
    rows, depth = rows_here[0].shape[0], proj.shape[0] // 8
    width = image.shape[1]
    half = width // 2
    ahead = is_ahead(x, core)
    for side, blocks in enumerate((rows_here, rows_there)):
        for block, *steps in zip(blocks, *ROW_STEPS):
            step = jnp.where(ahead, steps[side], steps[1 - side])
            start = pl.multiple_of(((z ^ step) * 2 + (core ^ side)) * rows, 8)
            image[pl.ds(start, rows), :] = block[:, :width].astype(F32)
            text[pl.ds(start, rows), :] = block[:, width : 2 * width].astype(F32)
            hidden[pl.ds(start, rows), :] = block[:, 2 * width :].astype(F32)
    for at, blocks in enumerate(projs):
        side, kind = divmod(at, len(PROJ_STEPS))
        left = pl.multiple_of((core ^ side) * half, 128)
        steps, column = PROJ_STEPS[kind]
        for block, step in enumerate(steps):
            start = pl.multiple_of(((z ^ step) * 2 + (x ^ column)) * depth, 16)
            proj[pl.ds(start, depth), pl.ds(left, half)] = blocks[block]
    hidden_short = hidden[...].astype(BF16)
    text[...] += jnp.dot(hidden_short, proj[...], preferred_element_type=F32)
    hidden_t[...] = hidden[...].T
    text_inv = inverse_norm(text[...])
    text_short = (text[...] * text_inv).astype(BF16)
    image_inv = inverse_norm(image[...])
    norms[...] = jnp.broadcast_to(image_inv, norms.shape)
    image_short = (image[...] * image_inv).astype(BF16)
    scale = jnp.exp(jnp.full((1, 1), log_scale[0], F32))
    logits = scale * lax.dot_general(
        image_short, text_short, ROWWISE, preferred_element_type=F32
    )
    row_max = jnp.max(logits, axis=1, keepdims=True)
    row_lse = row_max + jnp.log(jnp.sum(jnp.exp(logits - row_max), axis=1, keepdims=True))
    col_max = jnp.max(logits, axis=0, keepdims=True)
    col_lse = col_max + jnp.log(jnp.sum(jnp.exp(logits - col_max), axis=0, keepdims=True))
    eye = (
        lax.broadcasted_iota(jnp.int32, logits.shape, 0)
        == lax.broadcasted_iota(jnp.int32, logits.shape, 1)
    ).astype(F32)
    coef = factor * (jnp.exp(logits - row_lse) + jnp.exp(logits - col_lse) - 2.0 * eye)
    loss = factor * (
        jnp.sum(row_lse, axis=0, keepdims=True)
        + jnp.sum(col_lse, axis=1, keepdims=True)
        - 2.0 * jnp.sum(jnp.sum(eye * logits, axis=1, keepdims=True), axis=0, keepdims=True)
    )
    scale_grad = jnp.sum(jnp.sum(coef * logits, axis=1, keepdims=True), axis=0, keepdims=True)
    coefs[...] = coef
    own = pl.multiple_of((z * 2 + core) * rows, 8)
    grad_unit = scale * jnp.dot(
        coefs[pl.ds(own, rows), :].astype(BF16), text_short, preferred_element_type=F32
    )
    inverse = norms[pl.ds(own, rows), :1]
    unit = image[pl.ds(own, rows), :] * inverse
    grads[0] = (
        (grad_unit - unit * jnp.sum(unit * grad_unit, axis=-1, keepdims=True)) * inverse
    ).astype(BF16)
    grad_unit = scale * jnp.dot(coef.T.astype(BF16), image_short, preferred_element_type=F32)
    unit = text[...] * text_inv
    grad_all[...] = (
        grad_unit - unit * jnp.sum(unit * grad_unit, axis=-1, keepdims=True)
    ) * text_inv
    grads[1] = grad_all[pl.ds(own, rows), :].astype(BF16)
    share[...] = jnp.dot(
        hidden_t[pl.ds(pl.multiple_of(z * 2 * depth, 8), 2 * depth), :].astype(BF16),
        grad_all[:, pl.ds(pl.multiple_of(core * half, 128), half)].astype(BF16),
        preferred_element_type=F32,
    )
    totals = lanes_of(in_parts(loss) + in_parts(scale_grad), 2 * y + x, (8, half))
    for part, at in ((keep, x), (send, 1 - x)):
        rows_of = share[pl.ds(pl.multiple_of(at * depth, 8), depth), :]
        part[...] = jnp.concatenate([rows_of, totals]).astype(BF16)


def on_device_whole_group(image_embed, text_hidden, text_rest, proj_window, log_scale):
    rows, width = image_embed.shape[1:]
    depth = proj_window.shape[0]
    total_rows, total_depth, half = rows * 8, depth * 8, width // 2
    factor = 1.0 / (2.0 * total_rows * lax.axis_size("rep"))
    z, x, y, core = own_place()
    ahead = is_ahead(x, core)
    (own,) = lax.optimization_barrier((lax.dynamic_slice_in_dim(proj_window, core * half, half, 1),))
    samples = jnp.concatenate([image_embed[0], text_rest[0], text_hidden[0]], axis=1)
    far = z_far(own)
    even = jnp.stack([own, far])
    first = first_move(samples)
    own_rows = jnp.where(ahead, samples, first)
    near = z_near(own)[None]
    second = second_move(*after(far, own_rows))
    last = z_near(far)[None]
    even_x = x_peer(*after(near, even))
    third = z_near(first)
    odd_x = x_peer(jnp.concatenate([near, last]))
    fourth = jnp.where(ahead, first, fourth_move(second))
    there_01 = core_peer(jnp.stack(after(odd_x, own_rows, second)))
    there_third = core_peer(third)
    there_fourth = core_peer(fourth)
    proj_early = core_peer(jnp.concatenate([even, near, last, even_x]))
    proj_late = core_peer(*after(third, odd_x))
    rows_here = own_rows, second, third, fourth
    rows_there = there_01[0], there_01[1], there_third, there_fourth
    proj_here = even, near, last, even_x, odd_x
    proj_there = proj_early[0:2], proj_early[2:3], proj_early[3:4], proj_early[4:6], proj_late
    arrived = rows_here + rows_there + proj_here + proj_there
    keep, send, grads = pl.pallas_call(
        functools.partial(group_kernel, factor),
        out_shape=(
            jax.ShapeDtypeStruct((depth + 8, half), BF16),
            jax.ShapeDtypeStruct((depth + 8, half), BF16),
            jax.ShapeDtypeStruct((2, rows, width), BF16),
        ),
        in_specs=[IN_SMEM] + [IN_VMEM] * len(arrived),
        out_specs=[IN_VMEM] * 3,
        scratch_shapes=[
            pltpu.VMEM((total_rows, width), F32),
            pltpu.VMEM((total_rows, width), F32),
            pltpu.VMEM((total_rows, total_depth), F32),
            pltpu.VMEM((total_depth, total_rows), F32),
            pltpu.VMEM((total_rows, 128), F32),
            pltpu.VMEM((total_depth, width), BF16),
            pltpu.VMEM((total_rows, total_rows), F32),
            pltpu.VMEM((total_rows, width), F32),
            pltpu.VMEM((2 * depth, half), F32),
        ],
        compiler_params=pltpu.CompilerParams(vmem_limit_bytes=40 * 2**20),
        name="group_kernel",
    )(
        log_scale,
        *arrived
    )
    over_y, over_x, over_both = y_peer(keep), x_peer(send), xy_peer(send)
    grads = jnp.where(ahead, grads, trade_back(grads))
    share = (keep.astype(F32) + over_y.astype(F32)) + (over_x.astype(F32) + over_both.astype(F32))
    ours = share[:depth]
    theirs = core_peer(ours)
    grad_proj = jnp.where(
        core == 0,
        jnp.concatenate([ours, theirs], axis=1),
        jnp.concatenate([theirs, ours], axis=1),
    )
    totals = jnp.sum(share[depth, :24].reshape(2, 12), axis=1)
    return totals[0:1], totals[1:2], grads[0][None], grads[1][None], grad_proj


def solution(mesh):
    sizes = dict(mesh.shape)
    whole_group = sizes["blk"] == 8 and sizes["rep"] == 4
    return jax.shard_map(
        on_device_whole_group if whole_group else on_device,
        mesh=mesh,
        in_specs=(
            P("rep", "blk", None),
            P("rep", "blk", None),
            P("rep", "blk", None),
            P("blk", None),
            P(),
        ),
        out_specs=(P(), P(), P("rep", "blk", None), P("rep", "blk", None), P("blk", None)),
        check_vma=False,
    )
```

```python
import functools

import jax
import jax.numpy as jnp
from jax import lax
from jax.experimental import pallas as pl
from jax.experimental.pallas import tpu as pltpu
from jax.sharding import PartitionSpec as P


def joined(value, axis, join):
    pieces = jax.tree.map(lambda part: lax.all_gather(part, axis), value)
    head = jax.tree.map(lambda part: part[0], pieces)
    tail = jax.tree.map(lambda part: part[1:], pieces)
    running, _ = lax.scan(lambda running, slab: (join(running, slab), None), head, tail)
    return running


def unit_rows(values):
    row_norm = jnp.sqrt(jnp.sum(values * values, axis=-1, keepdims=True) + 1e-06)
    return (values / row_norm, row_norm)


def unit_back(unit_vec, row_norm, grad_unit):
    return (grad_unit - unit_vec * jnp.sum(unit_vec * grad_unit, axis=-1, keepdims=True)) / row_norm


def pair_products(left, right):
    return lax.dot_general(
        left, right, (((1,), (1,)), ((), ())), preferred_element_type=jnp.float32
    )


def combine_parts(earlier, later):
    col_top = jnp.maximum(earlier[0], later[0])
    return (
        col_top,
        earlier[1] * jnp.exp(earlier[0] - col_top) + later[1] * jnp.exp(later[0] - col_top),
    )


def on_device(image_embed, text_hidden, text_rest, proj_window, log_scale):
    hidden = text_hidden[0]
    local_rows = hidden.shape[0]
    group_rows = local_rows * lax.axis_size("blk")
    offset = lax.axis_index("blk") * local_rows
    factor = 1.0 / (2.0 * group_rows * lax.axis_size("rep"))
    logit_scale = jnp.exp(log_scale[0])
    columns = hidden
    projected = jnp.dot(
        columns,
        lax.all_gather(proj_window, "blk", axis=0, tiled=True),
        preferred_element_type=jnp.float32,
    )
    text_unit, text_norm = unit_rows(text_rest[0].astype(jnp.float32) + projected)
    image_unit, image_norm = unit_rows(image_embed[0].astype(jnp.float32))
    text_short = text_unit.astype(jnp.bfloat16)
    image_short = image_unit.astype(jnp.bfloat16)
    all_text = lax.all_gather(text_short, "blk", axis=0, tiled=True)
    logits = logit_scale * pair_products(image_short, all_text)
    row_lse = jax.nn.logsumexp(logits, axis=1)
    col_max = jnp.max(logits, axis=0)
    col_sum = jnp.sum(jnp.exp(logits - col_max[None, :]), axis=0)
    col_top, col_total = joined((col_max, col_sum), "blk", combine_parts)
    col_lse = col_top + jnp.log(col_total)
    positions = lax.broadcasted_iota(jnp.int32, (local_rows, group_rows), 1)
    own_rows = lax.broadcasted_iota(jnp.int32, (local_rows, group_rows), 0) + offset
    diagonal_mask = (positions == own_rows).astype(jnp.float32)
    own_col = lax.dynamic_slice_in_dim(col_lse, offset, local_rows, 0)
    loss_local = factor * (
        jnp.sum(row_lse) + jnp.sum(own_col) - 2.0 * jnp.sum(diagonal_mask * logits)
    )
    coef_image = factor * (
        jnp.exp(logits - row_lse[:, None])
        + jnp.exp(logits - col_lse[None, :])
        - 2.0 * diagonal_mask
    )
    scale_local = jnp.sum(coef_image * logits)
    grad_image_unit = logit_scale * jnp.dot(
        coef_image.astype(jnp.bfloat16), all_text, preferred_element_type=jnp.float32
    )
    grad_image = unit_back(image_unit, image_norm, grad_image_unit).astype(jnp.bfloat16)
    row_all = lax.all_gather(row_lse, "blk", axis=0, tiled=True)
    all_image = lax.all_gather(image_short, "blk", axis=0, tiled=True)
    cross_logits = logit_scale * pair_products(text_short, all_image)
    coef_text = factor * (
        jnp.exp(cross_logits - row_all[None, :])
        + jnp.exp(cross_logits - own_col[:, None])
        - 2.0 * diagonal_mask
    )
    grad_text_unit = logit_scale * jnp.dot(
        coef_text.astype(jnp.bfloat16), all_image, preferred_element_type=jnp.float32
    )
    grad_text = unit_back(text_unit, text_norm, grad_text_unit).astype(jnp.bfloat16)
    columns = hidden
    grad_share = lax.psum_scatter(
        lax.dot_general(
            columns, grad_text, (((0,), (0,)), ((), ())), preferred_element_type=jnp.float32
        ),
        "blk",
        scatter_dimension=0,
        tiled=True,
    )
    grad_proj = lax.psum(grad_share, "rep")
    loss_value, scale_grad = lax.psum((loss_local, scale_local), ("blk", "rep"))
    return (
        loss_value.reshape(1),
        scale_grad.reshape(1),
        grad_image[None],
        grad_text[None],
        grad_proj,
    )


F32 = jnp.float32
BF16 = jnp.bfloat16
ROWWISE = (((1,), (1,)), ((), ()))
IN_VMEM = pl.BlockSpec(memory_space=pltpu.VMEM)
IN_SMEM = pl.BlockSpec(memory_space=pltpu.SMEM)
ROW_STEPS = ((0, 1, 3, 2), (0, 2, 1, 3))
PROJ_STEPS = (((0, 2), 0), ((1,), 0), ((3,), 0), ((0, 2), 1), ((1, 3), 1))

def number(z, x, y, core):
    return (z * 2 + x) * 4 + y * 2 + core


def after(done, *values):
    return lax.optimization_barrier((values, done))[0]


def own_place():
    blk, rep = lax.axis_index("blk"), lax.axis_index("rep")
    return blk // 2, blk % 2, rep // 2, rep % 2


def moved(value, to):
    places = [(z, x, y, core) for z in range(4) for x in range(2) for y in range(2) for core in range(2)]
    return lax.ppermute(
        value, ("blk", "rep"), [(number(*place), number(*to(*place))) for place in places]
    )


def z_near(value):
    return moved(value, lambda z, x, y, core: (z ^ 1, x, y, core))


def z_far(value):
    return moved(value, lambda z, x, y, core: (z ^ 2, x, y, core))


def x_peer(value):
    return moved(value, lambda z, x, y, core: (z, 1 - x, y, core))


def y_peer(value):
    return moved(value, lambda z, x, y, core: (z, x, 1 - y, core))


def xy_peer(value):
    return moved(value, lambda z, x, y, core: (z, 1 - x, 1 - y, core))


def core_peer(value):
    return moved(value, lambda z, x, y, core: (z, x, y, 1 - core))


def is_ahead(x, core):
    return x == core


def trade(z, x, y, core):
    return z, core, y, x


def first_move(value):
    return moved(value, lambda z, x, y, core: (z ^ 2, x, y, core) if is_ahead(x, core) else trade(z, x, y, core))


def second_move(value):
    return moved(value, lambda z, x, y, core: (z ^ 1 if is_ahead(x, core) else z ^ 2, x, y, core))


def fourth_move(value):
    return moved(value, lambda z, x, y, core: (z, 1 - x, y, 1 - core) if is_ahead(x, core) else (z ^ 1, x, y, core))


def trade_back(value):
    return moved(value, lambda z, x, y, core: (z ^ 1, x, y, core) if is_ahead(x, core) else trade(z, x, y, core))


def in_parts(value):
    high = value.astype(BF16)
    rest = value - high.astype(F32)
    middle = rest.astype(BF16)
    return high, middle, (rest - middle.astype(F32)).astype(BF16)


def lanes_of(values, group, shape):
    lane = lax.broadcasted_iota(jnp.int32, shape, 1)
    row = jnp.zeros(shape, F32)
    for at, value in enumerate(values):
        row = jnp.where(lane == at * 4 + group, value.astype(F32), row)
    return row


def inverse_norm(values):
    return lax.rsqrt(jnp.sum(values * values, axis=-1, keepdims=True) + 1e-06)


def group_kernel(factor, log_scale, *refs):
    count = 2 * len(PROJ_STEPS)
    rows_here, rows_there, projs = refs[:4], refs[4:8], refs[8 : 8 + count]
    keep, send, grads = refs[8 + count : 11 + count]
    image, text, hidden, hidden_t, norms, proj, coefs, grad_all, share = refs[11 + count :]
    z, x, y, core = own_place()
    rows, depth = rows_here[0].shape[0], proj.shape[0] // 8
    width = image.shape[1]
    half = width // 2
    ahead = is_ahead(x, core)
    for side, blocks in enumerate((rows_here, rows_there)):
        for block, *steps in zip(blocks, *ROW_STEPS):
            step = jnp.where(ahead, steps[side], steps[1 - side])
            start = pl.multiple_of(((z ^ step) * 2 + (core ^ side)) * rows, 8)
            image[pl.ds(start, rows), :] = block[:, :width].astype(F32)
            text[pl.ds(start, rows), :] = block[:, width : 2 * width].astype(F32)
            hidden[pl.ds(start, rows), :] = block[:, 2 * width :].astype(F32)
    for at, blocks in enumerate(projs):
        side, kind = divmod(at, len(PROJ_STEPS))
        left = pl.multiple_of((core ^ side) * half, 128)
        steps, column = PROJ_STEPS[kind]
        for block, step in enumerate(steps):
            start = pl.multiple_of(((z ^ step) * 2 + (x ^ column)) * depth, 16)
            proj[pl.ds(start, depth), pl.ds(left, half)] = blocks[block]
    hidden_short = hidden[...].astype(BF16)
    text[...] += jnp.dot(hidden_short, proj[...], preferred_element_type=F32)
    hidden_t[...] = hidden[...].T
    text_inv = inverse_norm(text[...])
    text_short = (text[...] * text_inv).astype(BF16)
    image_inv = inverse_norm(image[...])
    norms[...] = jnp.broadcast_to(image_inv, norms.shape)
    image_short = (image[...] * image_inv).astype(BF16)
    scale = jnp.exp(jnp.full((1, 1), log_scale[0], F32))
    logits = scale * lax.dot_general(
        image_short, text_short, ROWWISE, preferred_element_type=F32
    )
    row_max = jnp.max(logits, axis=1, keepdims=True)
    row_lse = row_max + jnp.log(jnp.sum(jnp.exp(logits - row_max), axis=1, keepdims=True))
    col_max = jnp.max(logits, axis=0, keepdims=True)
    col_lse = col_max + jnp.log(jnp.sum(jnp.exp(logits - col_max), axis=0, keepdims=True))
    eye = (
        lax.broadcasted_iota(jnp.int32, logits.shape, 0)
        == lax.broadcasted_iota(jnp.int32, logits.shape, 1)
    ).astype(F32)
    coef = factor * (jnp.exp(logits - row_lse) + jnp.exp(logits - col_lse) - 2.0 * eye)
    loss = factor * (
        jnp.sum(row_lse, axis=0, keepdims=True)
        + jnp.sum(col_lse, axis=1, keepdims=True)
        - 2.0 * jnp.sum(jnp.sum(eye * logits, axis=1, keepdims=True), axis=0, keepdims=True)
    )
    scale_grad = jnp.sum(jnp.sum(coef * logits, axis=1, keepdims=True), axis=0, keepdims=True)
    coefs[...] = coef
    own = pl.multiple_of((z * 2 + core) * rows, 8)
    grad_unit = scale * jnp.dot(
        coefs[pl.ds(own, rows), :].astype(BF16), text_short, preferred_element_type=F32
    )
    inverse = norms[pl.ds(own, rows), :1]
    unit = image[pl.ds(own, rows), :] * inverse
    grads[0] = (
        (grad_unit - unit * jnp.sum(unit * grad_unit, axis=-1, keepdims=True)) * inverse
    ).astype(BF16)
    grad_unit = scale * jnp.dot(coef.T.astype(BF16), image_short, preferred_element_type=F32)
    unit = text[...] * text_inv
    grad_all[...] = (
        grad_unit - unit * jnp.sum(unit * grad_unit, axis=-1, keepdims=True)
    ) * text_inv
    grads[1] = grad_all[pl.ds(own, rows), :].astype(BF16)
    share[...] = jnp.dot(
        hidden_t[pl.ds(pl.multiple_of(z * 2 * depth, 8), 2 * depth), :].astype(BF16),
        grad_all[:, pl.ds(pl.multiple_of(core * half, 128), half)].astype(BF16),
        preferred_element_type=F32,
    )
    totals = lanes_of(in_parts(loss) + in_parts(scale_grad), 2 * y + x, (8, half))
    for part, at in ((keep, x), (send, 1 - x)):
        rows_of = share[pl.ds(pl.multiple_of(at * depth, 8), depth), :]
        part[...] = jnp.concatenate([rows_of, totals]).astype(BF16)


def on_device_whole_group(image_embed, text_hidden, text_rest, proj_window, log_scale):
    rows, width = image_embed.shape[1:]
    depth = proj_window.shape[0]
    total_rows, total_depth, half = rows * 8, depth * 8, width // 2
    factor = 1.0 / (2.0 * total_rows * lax.axis_size("rep"))
    z, x, y, core = own_place()
    ahead = is_ahead(x, core)
    (own,) = lax.optimization_barrier((lax.dynamic_slice_in_dim(proj_window, core * half, half, 1),))
    samples = jnp.concatenate([image_embed[0], text_rest[0], text_hidden[0]], axis=1)
    far = z_far(own)
    even = jnp.stack([own, far])
    first = first_move(samples)
    own_rows = jnp.where(ahead, samples, first)
    near = z_near(own)[None]
    second = second_move(*after(far, own_rows))
    last = z_near(far)[None]
    even_x = x_peer(*after(near, even))
    third = z_near(first)
    odd_x = x_peer(jnp.concatenate([near, last]))
    fourth = jnp.where(ahead, first, fourth_move(second))
    there_01 = core_peer(jnp.stack(after(odd_x, own_rows, second)))
    there_third = core_peer(third)
    there_fourth = core_peer(*after(odd_x, fourth))
    proj_early = core_peer(jnp.concatenate([even, near, last, even_x]))
    proj_late = core_peer(*after(third, odd_x))
    rows_here = own_rows, second, third, fourth
    rows_there = there_01[0], there_01[1], there_third, there_fourth
    proj_here = even, near, last, even_x, odd_x
    proj_there = proj_early[0:2], proj_early[2:3], proj_early[3:4], proj_early[4:6], proj_late
    arrived = rows_here + rows_there + proj_here + proj_there
    keep, send, grads = pl.pallas_call(
        functools.partial(group_kernel, factor),
        out_shape=(
            jax.ShapeDtypeStruct((depth + 8, half), BF16),
            jax.ShapeDtypeStruct((depth + 8, half), BF16),
            jax.ShapeDtypeStruct((2, rows, width), BF16),
        ),
        in_specs=[IN_SMEM] + [IN_VMEM] * len(arrived),
        out_specs=[IN_VMEM] * 3,
        scratch_shapes=[
            pltpu.VMEM((total_rows, width), F32),
            pltpu.VMEM((total_rows, width), F32),
            pltpu.VMEM((total_rows, total_depth), F32),
            pltpu.VMEM((total_depth, total_rows), F32),
            pltpu.VMEM((total_rows, 128), F32),
            pltpu.VMEM((total_depth, width), BF16),
            pltpu.VMEM((total_rows, total_rows), F32),
            pltpu.VMEM((total_rows, width), F32),
            pltpu.VMEM((2 * depth, half), F32),
        ],
        compiler_params=pltpu.CompilerParams(vmem_limit_bytes=40 * 2**20),
        name="group_kernel",
    )(
        log_scale,
        *arrived
    )
    over_y, over_x, over_both = y_peer(keep), x_peer(send), xy_peer(send)
    grads = jnp.where(ahead, grads, trade_back(grads))
    share = (keep.astype(F32) + over_y.astype(F32)) + (over_x.astype(F32) + over_both.astype(F32))
    ours = share[:depth]
    theirs = core_peer(ours)
    grad_proj = jnp.where(
        core == 0,
        jnp.concatenate([ours, theirs], axis=1),
        jnp.concatenate([theirs, ours], axis=1),
    )
    totals = jnp.sum(share[depth, :24].reshape(2, 12), axis=1)
    return totals[0:1], totals[1:2], grads[0][None], grads[1][None], grad_proj


def solution(mesh):
    sizes = dict(mesh.shape)
    whole_group = sizes["blk"] == 8 and sizes["rep"] == 4
    return jax.shard_map(
        on_device_whole_group if whole_group else on_device,
        mesh=mesh,
        in_specs=(
            P("rep", "blk", None),
            P("rep", "blk", None),
            P("rep", "blk", None),
            P("blk", None),
            P(),
        ),
        out_specs=(P(), P(), P("rep", "blk", None), P("rep", "blk", None), P("blk", None)),
        check_vma=False,
    )
```
